256 devices in a mesh: row: 16 (over y, x_lo, core), col: 16 (over x_hi, z).
Axes of the slice: x: 4 (x_hi: 2, x_lo: 2; x = x_hi * 2 + x_lo), y: 4, z: 8, core: 2. Of those that a mesh axis runs over, the one named last changes fastest.
Arguments:
- classes: int32 [256, 256], P('row', 'col'), may hold values from 0 to 15
- features: bfloat16 [256, 256, 128], P('row', 'col'), may hold values from -6 to 6
- cotangent: bfloat16 [256, 256, 128], P('row', 'col'), may hold values from -6 to 6
- table: float32 [16, 128], replicated, may hold values from -6 to 6
- norm_gain: float32 [128], replicated, may hold values from 0.5 to 1.5
- in_weight: bfloat16 [128, 512], replicated, may hold values from -0.5 to 0.5
- scan_weight: bfloat16 [256, 160], replicated, may hold values from -0.375 to 0.375
- step_weight: float32 [4, 8, 256], replicated, may hold values from -2 to 2
- step_bias: float32 [4, 256], replicated, may hold values from -6 to -2.5
- decay_log: float32 [4, 16, 256], replicated, may hold values from -4 to 2
- skip_gain: float32 [4, 256], replicated, may hold values from 0.5 to 1.5
- output_gain: float32 [256], replicated, may hold values from 0.5 to 1.5
- output_weight: bfloat16 [256, 128], replicated, may hold values from -0.375 to 0.375
Outputs:
- feature_grad: bfloat16 [256, 256, 128], P('row', 'col')
- in_weight_grad: float32 [128, 512], replicated
- scan_weight_grad: float32 [256, 160], replicated
- step_weight_grad: float32 [4, 8, 256], replicated
- step_bias_grad: float32 [4, 256], replicated
- decay_log_grad: float32 [4, 16, 256], replicated
- skip_gain_grad: float32 [4, 256], replicated
- norm_gain_grad: float32 [128], replicated
- output_gain_grad: float32 [256], replicated
- output_weight_grad: float32 [256, 128], replicated
The draws below stay inside these ranges and needn't reach their ends.
All inputs are finite; a program needn't handle non-finite values.
Results may differ from the reference program's by a relative error of at most 0.0076.
Values sent between devices are 32-bit elements; how exact they have to be, the bound alone decides.
No kernel may reach another device: no remote copies, remote signals or barrier semaphores. Data moves between devices by JAX's collectives and lax.ppermute only.
A program may use at most 320 MiB of HBM per device.

```python
import math
import jax
import jax.numpy as jnp
import numpy as np
from jax import lax

D = 128
E = 256
STATE = 16
RANK = 8
CLASSES = 16
TILE = 16
HEIGHT = 256
WIDTH = 256
TOKENS = 65536


def touch_ends(drawn, rng, least, high):
    index_at = [jax.random.randint(jax.random.fold_in(rng, axis), (), 0, length) for axis, length in enumerate(drawn.shape)]
    widest = drawn.shape.index(max(drawn.shape))
    beside = index_at[:widest] + [(index_at[widest] + 1) % drawn.shape[widest]] + index_at[widest + 1:]
    return drawn.at[tuple(index_at)].set(least).at[tuple(beside)].set(high)


def shard_levels(rng, shape, shards, low, largest):
    def one(position, parts):
        steps = jax.random.uniform(jax.random.fold_in(jax.random.fold_in(rng, 6), position), (parts,), jnp.float32, low / len(shards), largest / len(shards))
        return jnp.repeat(jnp.exp(steps), shape[position] // parts).reshape((-1,) + (1,) * (len(shape) - position - 1))

    level = one(*shards[0])
    for cut in shards[1:]:
        level = level * one(*cut)
    return level


def cumulative_ranks(amount, skew):
    portions = [(1 << 20) // math.isqrt(rank ** skew) + 1 for rank in range(1, amount + 1)]
    scale = 1 + sum(portions) // (1 << 30)
    return np.cumsum(np.array([max(1, weight // scale) for weight in portions]))


def skewed_ids(own_key, shape, count, lean):
    table = cumulative_ranks(count, lean)
    lot = jax.random.randint(jax.random.fold_in(own_key, 1), shape, 0, int(table[count - 1]))
    grade = jnp.searchsorted(jnp.asarray(table, jnp.int32), lot, side="right")
    return jax.random.permutation(jax.random.fold_in(own_key, 2), count)[grade].astype(jnp.int32)


def normal_values(stream_key, extent, scale, limit, split=(), held_as=jnp.bfloat16):
    values = jax.random.normal(stream_key, extent, jnp.float32) * scale
    if len(split) > 0:
        values = shard_levels(stream_key, extent, split, -0.22, 0.18) * values
    return jnp.clip(values, min=-limit, max=limit).astype(held_as)


def setup_inputs(seed: int = 0) -> dict:
    arg_keys = jax.random.split(jax.random.key(seed), 14)
    classes = touch_ends(skewed_ids(arg_keys[0], (HEIGHT, WIDTH), CLASSES, 2), jax.random.fold_in(arg_keys[0], 3), 0, CLASSES - 1).astype(jnp.int32)
    features = normal_values(arg_keys[1], (HEIGHT, WIDTH, D), 1.0, 6.0, ((0, 16), (1, 16)))
    cotangent = normal_values(arg_keys[2], (HEIGHT, WIDTH, D), 1.0, 6.0, ((0, 16), (1, 16)))
    table = normal_values(arg_keys[3], (CLASSES, D), 1.0, 6.0, (), jnp.float32)
    norm_gain = jnp.clip(1.0 + 0.1 * jax.random.normal(arg_keys[4], (D,), jnp.float32), 0.5, 1.5)
    in_weight = normal_values(arg_keys[5], (D, 2 * E), D ** -0.5, 0.5)
    scan_weight = normal_values(arg_keys[6], (E, 4 * (RANK + 2 * STATE)), E ** -0.5, 0.375)
    step_weight = normal_values(arg_keys[7], (4, RANK, E), RANK ** -0.5, 2.0, (), jnp.float32)
    step_bias = jnp.clip(jax.random.uniform(arg_keys[8], (4, E), jnp.float32, -6.0, -2.5), -6.0, -2.5)
    decay_log = jnp.clip(jax.random.uniform(arg_keys[9], (4, STATE, E), jnp.float32, -4.0, 2.0), -4.0, 2.0)
    skip_gain = jnp.clip(jax.random.uniform(arg_keys[10], (4, E), jnp.float32, 0.5, 1.5), 0.5, 1.5)
    output_gain = jnp.clip(1.0 + 0.1 * jax.random.normal(arg_keys[11], (E,), jnp.float32), 0.5, 1.5)
    output_weight = normal_values(arg_keys[12], (E, D), E ** -0.5, 0.375)
    return {"classes": classes, "features": features, "cotangent": cotangent, "table": table, "norm_gain": norm_gain, "in_weight": in_weight, "scan_weight": scan_weight, "step_weight": step_weight, "step_bias": step_bias, "decay_log": decay_log, "skip_gain": skip_gain, "output_gain": output_gain, "output_weight": output_weight}


EPS = 1e-05
HIGHEST = lax.Precision.HIGHEST

def layer_norm(rows, gain):
    average = lax.optimization_barrier(jnp.mean(rows, axis=-1, keepdims=True))
    centred = rows - average
    spread = lax.optimization_barrier(jnp.mean(centred * centred, axis=-1, keepdims=True))
    return centred * lax.rsqrt(spread + EPS) * gain

def silu_slope(before):
    sigma = jax.nn.sigmoid(before)
    return sigma * (1.0 + before * (1.0 - sigma))

def embed(features, classes, table):
    labels = jnp.arange(table.shape[0], dtype=jnp.int32)
    onehot = (classes[..., None] == labels).astype(jnp.float32)
    lookup = jnp.einsum('hwk,kd->hwd', onehot, table.astype(jnp.float32), precision=HIGHEST)
    return features.astype(jnp.float32) + lookup

def direction_inputs(projected, step_weight, step_bias):
    rank = step_weight.shape[1]
    group = projected.shape[1] // 4
    states = (group - rank) // 2
    steps, inflow, readout = ([], [], [])
    for direction in range(4):
        first = direction * group
        lowrank = projected[:, first:first + rank]
        before = jnp.dot(lowrank, step_weight[direction], precision=HIGHEST) + step_bias[direction]
        steps.append(jax.nn.softplus(before))
        inflow.append(projected[:, first + rank:first + rank + states])
        readout.append(projected[:, first + rank + states:first + group])
    return (jnp.stack(steps), jnp.stack(inflow), jnp.stack(readout))

def gate_output(total, gate_in, output_gain):
    return layer_norm(total, output_gain) * jax.nn.silu(gate_in)

def to_sequence(grid, direction):
    if direction < 2:
        grid = jnp.transpose(grid, (1, 0, 2))
    if direction % 2 == 1:
        grid = grid[::-1]
    return grid

def from_sequence(lines, direction):
    if direction % 2 == 1:
        lines = lines[::-1]
    if direction < 2:
        lines = jnp.transpose(lines, (1, 0, 2))
    return lines

def scan_lines(values, steps, inflow, readout, rate, skip, start):

    def advance(state, slab):
        value, step, source, probe = slab
        decay = jnp.exp(step[:, None, :] * rate)
        state = decay * state + source[:, :, None] * (step * value)[:, None, :]
        output = jnp.einsum('bn,bne->be', probe, state, precision=HIGHEST) + skip * value
        return (state, output)
    final, outputs = lax.scan(advance, start, (values, steps, inflow, readout))
    return (outputs, final)

def reference(classes, features, cotangent, table, norm_gain, in_weight, scan_weight, step_weight, step_bias, decay_log, skip_gain, output_gain, output_weight):
    height, width, model_width = features.shape
    inner = output_weight.shape[0]
    count = height * width
    grad_scale = float(TOKENS) ** (-0.5)
    embedded = embed(features, classes, table).reshape(count, model_width)
    normed = layer_norm(embedded, norm_gain).astype(jnp.bfloat16)
    mixed = jnp.dot(normed, in_weight, preferred_element_type=jnp.float32)
    values = jax.nn.silu(mixed[:, :inner]).astype(jnp.bfloat16)
    gate_in = mixed[:, inner:]
    projected = jnp.dot(values, scan_weight, preferred_element_type=jnp.float32)
    steps, inflow, readout = direction_inputs(projected, step_weight, step_bias)
    values_wide = values.astype(jnp.float32)

    def lines_of(flat, direction):
        return to_sequence(flat.reshape(height, width, flat.shape[-1]), direction)

    def flat_of(lines, direction):
        return from_sequence(lines, direction).reshape(count, lines.shape[-1])

    def run_lines(line_values, line_steps, line_inflow, line_readout, log_rate, skip):
        rate = -jnp.exp(log_rate)
        blocks = line_values.shape[0] // TILE

        def regroup(array):
            return array.reshape((blocks, TILE) + array.shape[1:])

        def block(state, slab):
            outputs, state = scan_lines(slab[0], slab[1], slab[2], slab[3], rate, skip, state)
            return (state, outputs)
        start = jnp.zeros((line_values.shape[1], rate.shape[0], rate.shape[1]), jnp.float32)
        unused, outputs = lax.scan(jax.checkpoint(block), start, (regroup(line_values), regroup(line_steps), regroup(line_inflow), regroup(line_readout)))
        return outputs.reshape(line_values.shape)
    total = jnp.zeros((count, inner), jnp.float32)
    pulls = []
    for direction in range(4):
        outputs, pull = jax.vjp(run_lines, lines_of(values_wide, direction), lines_of(steps[direction], direction), lines_of(inflow[direction], direction), lines_of(readout[direction], direction), decay_log[direction], skip_gain[direction])
        pulls.append(pull)
        total = total + flat_of(outputs, direction)
    gated = gate_output(total, gate_in, output_gain).astype(jnp.bfloat16)
    upstream = cotangent.reshape(count, model_width)
    output_weight_grad = jnp.dot(gated.T, upstream, preferred_element_type=jnp.float32)
    d_gated = jnp.dot(upstream, output_weight.T, preferred_element_type=jnp.float32)
    unused, gate_pull = jax.vjp(gate_output, total, gate_in, output_gain)
    d_total, d_gate_in, output_gain_grad = gate_pull(d_gated)
    d_values_scan = jnp.zeros((count, inner), jnp.float32)
    d_steps, d_inflow, d_readout, decay_grads, skip_grads = ([], [], [], [], [])
    for direction in range(4):
        grads = pulls[direction](lines_of(d_total, direction))
        d_values_scan = d_values_scan + flat_of(grads[0], direction)
        d_steps.append(flat_of(grads[1], direction))
        d_inflow.append(flat_of(grads[2], direction))
        d_readout.append(flat_of(grads[3], direction))
        decay_grads.append(grads[4])
        skip_grads.append(grads[5])
    unused, input_pull = jax.vjp(direction_inputs, projected, step_weight, step_bias)
    d_projected, step_weight_grad, step_bias_grad = input_pull((jnp.stack(d_steps), jnp.stack(d_inflow), jnp.stack(d_readout)))
    d_projected = d_projected.astype(jnp.bfloat16)
    scan_weight_grad = jnp.dot(values.T, d_projected, preferred_element_type=jnp.float32)
    d_values = jnp.dot(d_projected, scan_weight.T, preferred_element_type=jnp.float32) + d_values_scan
    d_mixed = jnp.concatenate([d_values * silu_slope(mixed[:, :inner]), d_gate_in], axis=1).astype(jnp.bfloat16)
    in_weight_grad = jnp.dot(normed.T, d_mixed, preferred_element_type=jnp.float32)
    d_normed = jnp.dot(d_mixed, in_weight.T, preferred_element_type=jnp.float32)
    unused, norm_pull = jax.vjp(layer_norm, embedded, norm_gain)
    d_embedded, norm_gain_grad = norm_pull(d_normed)
    feature_grad = (upstream.astype(jnp.float32) + d_embedded).astype(jnp.bfloat16).reshape(height, width, model_width)
    return (feature_grad, in_weight_grad * grad_scale, scan_weight_grad * grad_scale, step_weight_grad * grad_scale, step_bias_grad * grad_scale, jnp.stack(decay_grads) * grad_scale, jnp.stack(skip_grads) * grad_scale, norm_gain_grad * grad_scale, output_gain_grad * grad_scale, output_weight_grad * grad_scale)
```

```python
import functools

import jax
import jax.numpy as jnp
from jax import lax
from jax.experimental import pallas as pl
from jax.experimental.pallas import tpu as pltpu
from jax.sharding import PartitionSpec as P

EPS = 1e-05
HIGHEST = lax.Precision.HIGHEST
LOG2E = 1.4426950408889634
LN2 = 0.6931471805599453
CHUNKS = 8
LANES = 128
F32 = jnp.float32
BF16 = jnp.bfloat16
PARAMS = pltpu.CompilerParams(vmem_limit_bytes=48 * 1024 * 1024)


def normalise(rows):
    average = jnp.mean(rows, axis=-1, keepdims=True)
    centred = rows - average
    spread = jnp.mean(centred * centred, axis=-1, keepdims=True)
    inverse = lax.rsqrt(spread + EPS)
    return centred * inverse, inverse


def normalise_pull(upstream, unit, inverse):
    first = jnp.mean(upstream, axis=-1, keepdims=True)
    second = jnp.mean(upstream * unit, axis=-1, keepdims=True)
    return inverse * (upstream - first - unit * second)


def sigmoid(before):
    return 1.0 / (1.0 + jnp.exp(-before))


def softplus(before):
    return jnp.maximum(before, 0.0) + jnp.log1p(jnp.exp(-jnp.abs(before)))


def product(left, right, over=((1,), (0,)), precision=None):
    return lax.dot_general(left, right, (over, ((), ())), precision=precision, preferred_element_type=F32)


def embed_kernel(classes, features, table, embedded, turned, *, edge):
    labels = lax.broadcasted_iota(jnp.int32, (classes.shape[0], table.shape[0]), 1)
    onehot = (classes[...] == labels).astype(F32)
    cells = features[...].astype(F32) + product(onehot, table[...], precision=HIGHEST)
    embedded[...] = cells
    for row in range(edge):
        turned[pl.ds(row, edge, stride=edge), :] = cells[row * edge : (row + 1) * edge]


def chain_chunks(total, state, upward):
    place = lax.broadcasted_iota(jnp.int32, state.shape, 0)
    reach = 1
    while reach < CHUNKS:
        shift = reach if upward else CHUNKS - reach
        inside = place >= reach if upward else place < CHUNKS - reach
        state = state + total * jnp.where(inside, pltpu.roll(state, shift, 0), 0.0)
        total = total * jnp.where(inside, pltpu.roll(total, shift, 0), 1.0)
        reach *= 2
    shift = 1 if upward else CHUNKS - 1
    inside = place >= 1 if upward else place < CHUNKS - 1
    return jnp.where(inside, pltpu.roll(state, shift, 0), 0.0)


def spread_rates(decay_log, rates):
    for direction in range(2):
        scaled = -jnp.exp(decay_log[direction]) * LOG2E
        for entry in range(scaled.shape[0]):
            rates[direction, entry] = jnp.broadcast_to(
                scaled[entry : entry + 1], (CHUNKS, scaled.shape[1])
            )


def put_halves(target, rows):
    for half in range(target.shape[0]):
        target[half] = rows[:, half * LANES : (half + 1) * LANES]


def take_halves(source):
    return jnp.concatenate([source[half] for half in range(source.shape[0])], axis=1)


def load_interleaved(source):
    span = source.shape[0] // CHUNKS
    return jnp.concatenate(
        [source[pl.ds(place, CHUNKS, stride=span), :] for place in range(span)], axis=0
    )


def store_natural(target, rows):
    span = rows.shape[0] // CHUNKS
    for place in range(span):
        target[pl.ds(place, CHUNKS, stride=span), :] = rows[place * CHUNKS : (place + 1) * CHUNKS]


def sweep(span, advance, carried, unroll):
    def several(turn, state):
        for part in range(unroll):
            state = advance(turn * unroll + part, state)
        return state

    return lax.fori_loop(0, span // unroll, several, carried)


def expand_columns(flat, columns, rank, group):
    length, width = flat.shape
    wanted = group - rank
    padded = jnp.concatenate([flat, jnp.zeros((length, LANES - width), F32)], axis=1)
    high = padded.astype(BF16)
    low = (padded - high.astype(F32)).astype(BF16)
    both = jnp.concatenate([high, low], axis=1)
    row = lax.broadcasted_iota(jnp.int32, (2 * LANES, 2 * LANES), 0)
    lane = lax.broadcasted_iota(jnp.int32, (2 * LANES, 2 * LANES), 1)
    row = jnp.where(row >= LANES, row - LANES, row)
    offset = row - jnp.where(lane >= LANES, 1, 0)
    for direction in range(2):

        def one(pair, unused, direction=direction):
            chosen = (offset == direction * group + rank + 2 * pair).astype(F32).astype(BF16)
            wide = product(both, chosen)
            columns[direction * wanted + 2 * pair] = wide[:, :LANES]
            columns[direction * wanted + 2 * pair + 1] = wide[:, LANES:]
            return unused

        lax.fori_loop(0, wanted // 2, one, 0)


def sum_columns(terms, target, first):
    row = lax.broadcasted_iota(jnp.int32, (2 * LANES, LANES), 0)
    lane = lax.broadcasted_iota(jnp.int32, (2 * LANES, LANES), 1)
    offset = lane - jnp.where(row >= LANES, 1, 0)

    def one(pair, unused):
        chosen = (offset == first + 2 * pair).astype(F32).astype(BF16)
        both = jnp.concatenate([terms[2 * pair], terms[2 * pair + 1]], axis=1).astype(BF16)
        target[...] = target[...] + product(both, chosen)
        return unused

    lax.fori_loop(0, terms.shape[0] // 2, one, 0)


def slot(place):
    return pl.ds(pl.multiple_of(place * CHUNKS, CHUNKS), CHUNKS)


def forward_kernel(
    embedded,
    norm_gain,
    in_weight,
    scan_weight,
    step_weight,
    step_bias,
    decay_log,
    skip_gain,
    result,
    mixed_out,
    steps,
    projected,
    starts,
    values,
    rates,
    totals,
    natural,
    columns,
    *,
    rank,
    states,
):
    length, inner = result.shape
    halves = inner // LANES
    span = length // CHUNKS
    group = rank + 2 * states
    unit, unused = normalise(load_interleaved(embedded))
    normed = (unit * norm_gain[...]).astype(BF16)
    mixed = product(normed, in_weight[...])
    mixed_out[...] = mixed
    rounded = (mixed * sigmoid(mixed)).astype(BF16)
    flat = product(rounded, scan_weight[...])
    projected[...] = flat
    expand_columns(flat, columns, rank, group)
    wide = rounded.astype(F32)
    values[...] = wide
    totals[...] = wide * (skip_gain[0:1] + skip_gain[1:2])
    for direction in range(2):
        lowrank = flat[:, direction * group : direction * group + rank]
        before = (
            product(lowrank, step_weight[direction], precision=HIGHEST)
            + step_bias[direction : direction + 1]
        )
        steps[direction] = softplus(before)
    spread_rates(decay_log, rates)
    zero = jnp.zeros((CHUNKS, LANES), F32)

    for direction in range(2):
        source = direction * 2 * states
        probe = source + states

        def rows(turn, direction=direction):
            return slot(turn if direction == 0 else span - 1 - turn)

        for half in range(halves):
            lanes = slice(half * LANES, (half + 1) * LANES)

            def ending(turn, carried, direction=direction, lanes=lanes, rows=rows, source=source):
                state, total = carried
                at = rows(turn)
                step = steps[direction, at, lanes]
                drive = step * values[at, lanes]
                state = tuple(
                    jnp.exp2(step * rates[direction, n, :, lanes]) * state[n]
                    + columns[source + n, at, :] * drive
                    for n in range(states)
                )
                return (state, total + step)

            state, total = sweep(span, ending, ((zero,) * states, zero), 4)
            begin = []
            for n in range(states):
                factor = jnp.exp2(total * rates[direction, n, :, lanes])
                start = chain_chunks(factor, state[n], direction == 0)
                starts[direction, n, :, lanes] = start
                begin.append(start)

            def advance(
                turn, state, direction=direction, lanes=lanes, rows=rows, source=source, probe=probe
            ):
                at = rows(turn)
                step = steps[direction, at, lanes]
                drive = step * values[at, lanes]
                output = totals[at, lanes]
                after = []
                for n in range(states):
                    here = (
                        jnp.exp2(step * rates[direction, n, :, lanes]) * state[n]
                        + columns[source + n, at, :] * drive
                    )
                    output = output + columns[probe + n, at, :] * here
                    after.append(here)
                totals[at, lanes] = output
                return tuple(after)

            sweep(span, advance, tuple(begin), 4)
    for half in range(halves):
        store_natural(natural.at[half], totals[:, half * LANES : (half + 1) * LANES])
    result[...] = take_halves(natural)


def pack_sizes(inner, width, rank, states):
    halves = inner // LANES
    group = rank + 2 * states
    sizes = (halves * width, halves * 2 * group, halves * 2 * rank, halves * 2 * states, 8)
    firsts = [sum(sizes[:index]) for index in range(len(sizes) + 1)]
    return firsts


def pack_halves(target, first, rows):
    height, width = rows.shape
    for half in range(width // LANES):
        target[first + half * height : first + (half + 1) * height] = rows[
            :, half * LANES : (half + 1) * LANES
        ]


def gate_kernel(
    embedded,
    norm_gain,
    in_weight,
    output_gain,
    output_weight,
    cotangent,
    along_rows,
    along_cols,
    d_rows,
    d_cols,
    d_embedded,
    packed,
    turned,
    *,
    edge,
):
    inner, width = output_weight.shape
    halves = inner // LANES
    put_halves(turned, along_cols[...])
    total = along_rows[...] + jnp.concatenate(
        [
            jnp.concatenate(
                [turned[half, pl.ds(row, edge, stride=edge), :] for row in range(edge)], axis=0
            )
            for half in range(halves)
        ],
        axis=1,
    )
    base, inverse = normalise(embedded[...])
    gain = norm_gain[...]
    normed = (base * gain).astype(BF16)
    gate_in = product(normed, in_weight[...])
    sigma = sigmoid(gate_in)
    gate = gate_in * sigma
    slope = sigma * (1.0 + gate_in * (1.0 - sigma))
    unit, spread = normalise(total)
    strength = output_gain[...]
    gated = (unit * strength * gate).astype(BF16)
    upstream = cotangent[...]
    d_gated = product(upstream, output_weight[...], ((1,), (1,)))
    d_scaled = d_gated * gate
    d_total = normalise_pull(d_scaled * strength, unit, spread)
    d_rows[...] = d_total
    for half in range(halves):
        lanes = slice(half * LANES, (half + 1) * LANES)
        for row in range(edge):
            turned[half, pl.ds(row, edge, stride=edge), :] = d_total[
                row * edge : (row + 1) * edge, lanes
            ]
    d_cols[...] = take_halves(turned)
    d_gate = (d_gated * unit * strength * slope).astype(BF16)
    d_normed = product(d_gate, in_weight[...], ((1,), (1,)))
    d_embedded[...] = normalise_pull(d_normed * gain, base, inverse) + upstream.astype(F32)
    first = halves * width
    pack_halves(packed, 0, product(normed, d_gate, ((0,), (0,))))
    packed[first : first + inner] = product(gated, upstream, ((0,), (0,)))
    last = first + inner
    packed[last : last + 8] = jnp.zeros((8, LANES), F32)
    packed[last : last + 1] = jnp.sum(d_normed * base, axis=0, keepdims=True)
    pack_halves(packed, last + 1, jnp.sum(d_scaled * unit, axis=0, keepdims=True))


def backward_kernel(
    embedded,
    norm_gain,
    in_weight,
    scan_weight,
    step_weight,
    step_bias,
    decay_log,
    mixed_in,
    steps,
    projected,
    starts,
    upstream,
    skip_gain,
    d_embedded,
    packed,
    values,
    rates,
    history,
    decays,
    d_projected,
    d_values,
    d_steps,
    d_rates,
    enter,
    natural,
    arriving_lines,
    columns,
    terms,
    *,
    rank,
    states,
):
    length, inner = upstream.shape
    width = embedded.shape[1]
    halves = inner // LANES
    span = length // CHUNKS
    group = rank + 2 * states
    firsts = pack_sizes(inner, width, rank, states)
    mixed = mixed_in[...]
    sigma = sigmoid(mixed)
    rounded = (mixed * sigma).astype(BF16)
    wide = rounded.astype(F32)
    values[...] = wide
    put_halves(natural, upstream[...])
    incoming = jnp.concatenate(
        [load_interleaved(natural.at[half]) for half in range(halves)], axis=1
    )
    arriving_lines[...] = incoming
    d_values[...] = incoming * (skip_gain[0:1] + skip_gain[1:2])
    flat = projected[...]
    expand_columns(flat, columns, rank, group)
    d_projected[...] = jnp.zeros(d_projected.shape, F32)
    spread_rates(decay_log, rates)
    zero = jnp.zeros((CHUNKS, LANES), F32)
    packed[firsts[4] : firsts[5]] = jnp.zeros((8, LANES), F32)
    pack_halves(packed, firsts[4] + 1, jnp.sum(incoming * wide, axis=0, keepdims=True))

    for direction in range(2):
        source = direction * 2 * states
        probe = source + states
        d_rates[...] = jnp.zeros(d_rates.shape, F32)

        def rows(turn, direction=direction):
            return slot(turn if direction == 0 else span - 1 - turn)

        for half in range(halves):
            lanes = slice(half * LANES, (half + 1) * LANES)

            def advance(turn, carried, direction=direction, lanes=lanes, rows=rows, source=source):
                state, total = carried
                at = rows(turn)
                step = steps[direction, at, lanes]
                drive = step * values[at, lanes]
                after = []
                for n in range(states):
                    decay = jnp.exp2(step * rates[direction, n, :, lanes])
                    decays[turn, n, :, lanes] = decay
                    here = decay * state[n] + columns[source + n, at, :] * drive
                    history[turn + 1, n, :, lanes] = here
                    after.append(here)
                return (tuple(after), total + step)

            begin = tuple(starts[direction, n, :, lanes] for n in range(states))
            for n in range(states):
                history[0, n, :, lanes] = begin[n]
            unused, total = sweep(span, advance, (begin, zero), 4)

            def retreat(turn, carried, lanes=lanes, rows=rows, probe=probe):
                back = span - 1 - turn
                at = rows(back)
                arriving = arriving_lines[at, lanes]
                return tuple(
                    decays[back, n, :, lanes]
                    * (columns[probe + n, at, :] * arriving + carried[n])
                    for n in range(states)
                )

            carried = sweep(span, retreat, (zero,) * states, 4)
            for n in range(states):
                factor = jnp.exp2(total * rates[direction, n, :, lanes])
                enter[n, :, lanes] = chain_chunks(factor, carried[n], direction == 1)

        def pull(turn, carried, direction=direction, rows=rows, source=source, probe=probe):
            back = span - 1 - turn
            at = rows(back)
            step = steps[direction, at, :]
            value = values[at, :]
            drive = step * value
            arriving = arriving_lines[at, :]
            d_drive = jnp.zeros((CHUNKS, inner), F32)
            d_step = jnp.zeros((CHUNKS, inner), F32)
            after = []
            for n in range(states):
                reader = jnp.concatenate([columns[probe + n, at, :]] * halves, axis=1)
                writer = jnp.concatenate([columns[source + n, at, :]] * halves, axis=1)
                adjoint = reader * arriving + carried[n]
                leaving = decays[back, n] * adjoint
                after.append(leaving)
                d_probe = arriving * history[back + 1, n]
                d_source = adjoint * drive
                terms[n, at, :] = sum(
                    d_source[:, half * LANES : (half + 1) * LANES] for half in range(halves)
                )
                terms[states + n, at, :] = sum(
                    d_probe[:, half * LANES : (half + 1) * LANES] for half in range(halves)
                )
                d_drive = d_drive + adjoint * writer
                weight = leaving * history[back, n]
                d_step = d_step + weight * rates[direction, n]
                d_rates[n] = d_rates[n] + weight * step
            d_values[at, :] = d_values[at, :] + step * d_drive
            d_steps[at, :] = value * d_drive + LN2 * d_step
            return tuple(after)

        sweep(span, pull, tuple(enter[n] for n in range(states)), 1)
        first = direction * group
        sum_columns(terms, d_projected, first + rank)
        pack_halves(
            packed,
            firsts[3] + direction * halves * states,
            jnp.sum(d_rates[...], axis=1) * -jnp.exp(decay_log[direction]),
        )
        lowrank = flat[:, first : first + rank]
        before = (
            product(lowrank, step_weight[direction], precision=HIGHEST)
            + step_bias[direction : direction + 1]
        )
        d_before = d_steps[...] * sigmoid(before)
        pack_halves(
            packed,
            firsts[4] + 1 + halves * (1 + direction),
            jnp.sum(d_before, axis=0, keepdims=True),
        )
        pack_halves(
            packed,
            firsts[2] + direction * halves * rank,
            product(lowrank, d_before, ((0,), (0,)), HIGHEST),
        )
        d_projected[:, first : first + rank] = product(
            d_before, step_weight[direction], ((1,), (1,)), HIGHEST
        )

    unit, inverse = normalise(load_interleaved(embedded))
    gain = norm_gain[...]
    normed = (unit * gain).astype(BF16)
    d_flat = d_projected[:, : 2 * group].astype(BF16)
    pack_halves(packed, firsts[1], product(d_flat, rounded, ((0,), (0,))))
    d_all = product(d_flat, scan_weight[...], ((1,), (1,))) + d_values[...]
    d_mixed = (d_all * sigma * (1.0 + mixed * (1.0 - sigma))).astype(BF16)
    pack_halves(packed, 0, product(normed, d_mixed, ((0,), (0,))))
    d_normed = product(d_mixed, in_weight[...], ((1,), (1,)))
    packed[firsts[4] : firsts[4] + 1] = jnp.sum(d_normed * unit, axis=0, keepdims=True)
    store_natural(d_embedded, normalise_pull(d_normed * gain, unit, inverse))


def finish_kernel(own, along_rows, along_cols, gradient, turned, *, edge):
    turned[...] = along_cols[...].reshape(turned.shape)
    natural = jnp.concatenate(
        [turned[pl.ds(row, edge, stride=edge), :] for row in range(edge)], axis=0
    )
    gradient[...] = (own[...] + along_rows[...] + natural).astype(BF16)


def pack_kernel(gate, first, second, lines, blocks, stacked, *, shared):
    count, height, unused = blocks.shape
    edge = lines.shape[0] // count
    gate_rows, scan_rows = (gate.shape[0], first.shape[0])
    rest = scan_rows - shared
    stacked[:gate_rows] = gate[...]
    stacked[gate_rows : gate_rows + shared] = first[:shared] + second[:shared]
    start = gate_rows + shared
    stacked[start : start + rest] = first[shared:]
    stacked[start + rest : start + 2 * rest] = second[shared:]
    start = start + 2 * rest
    stacked[start:] = jnp.zeros((stacked.shape[0] - start, LANES), F32)
    for block in range(count):
        blocks[block, :edge] = lines[block * edge : (block + 1) * edge]
        blocks[block, edge:] = stacked[block * (height - edge) : (block + 1) * (height - edge)]


def unpack_kernel(
    whole,
    in_weight,
    scan_weight,
    step_weight,
    step_bias,
    decay,
    skip,
    norm_gain,
    output_gain,
    output_weight,
    *,
    scale,
    rank,
    states,
):
    width, double = in_weight.shape
    inner = double // 2
    halves = inner // LANES
    group = rank + 2 * states
    firsts = pack_sizes(inner, width, rank, states)
    shared = firsts[1]

    def joined(start, height):
        return scale * jnp.concatenate(
            [whole[start + half * height : start + (half + 1) * height] for half in range(halves)],
            axis=1,
        )

    gate = halves * width + inner + 8
    in_weight[:, inner:] = joined(0, width)
    in_weight[:, :inner] = joined(gate, width)
    output_weight[...] = scale * whole[halves * width : halves * width + inner]
    small = halves * width + inner
    output_gain[...] = joined(small + 1, 1)
    gains = whole[small : small + 1]
    projected = []
    for pair in range(2):
        start = gate + shared + pair * (firsts[5] - shared) - shared
        projected.append(joined(start + firsts[1], 2 * group))
        for direction in range(2):
            index = 2 * pair + direction
            step_weight[index] = joined(start + firsts[2] + direction * halves * rank, rank)
            decay[index] = joined(start + firsts[3] + direction * halves * states, states)
            base = start + firsts[4] + 1
            skip[index : index + 1] = joined(base, 1)
            step_bias[index : index + 1] = joined(base + halves * (1 + direction), 1)
        gains = gains + whole[start + firsts[4] : start + firsts[4] + 1]
    norm_gain[...] = scale * gains
    scan_weight[...] = jnp.concatenate(projected, axis=0).T


def shape_of(*sizes, dtype=F32):
    return jax.ShapeDtypeStruct(sizes, dtype)


def exchange(rows, axis):
    count = lax.axis_size(axis)
    length, width = rows.shape
    blocks = rows.reshape(count, length // count, width)
    return lax.all_to_all(blocks, axis, 0, 0).reshape(length, width)


def share(block, axis):
    count = lax.axis_size(axis)
    copies = jnp.broadcast_to(block[None], (count,) + block.shape)
    return lax.all_to_all(copies, axis, 0, 0)


def local(
    classes,
    features,
    cotangent,
    table,
    norm_gain,
    in_weight,
    scan_weight,
    step_weight,
    step_bias,
    decay_log,
    skip_gain,
    output_gain,
    output_weight,
):
    edge, across, width = features.shape
    inner = output_weight.shape[0]
    rank, states = (step_weight.shape[1], decay_log.shape[1])
    group = rank + 2 * states
    cells = edge * across
    span = cells // CHUNKS
    halves = inner // LANES
    scale = float(cells * lax.axis_size("row") * lax.axis_size("col")) ** (-0.5)
    gain = norm_gain.reshape(1, width)
    value_weight, gate_weight = (in_weight[:, :inner], in_weight[:, inner:])

    embedded, turned = pl.pallas_call(
        functools.partial(embed_kernel, edge=edge),
        out_shape=(shape_of(cells, width), shape_of(cells, width)),
        compiler_params=PARAMS,
        name="embed",
    )(classes.reshape(cells, 1), features.reshape(cells, width), table)

    forward = pl.pallas_call(
        functools.partial(forward_kernel, rank=rank, states=states),
        out_shape=(
            shape_of(cells, inner),
            shape_of(cells, inner),
            shape_of(2, cells, inner),
            shape_of(cells, 2 * group),
            shape_of(2, states, CHUNKS, inner),
        ),
        scratch_shapes=[
            pltpu.VMEM((cells, inner), F32),
            pltpu.VMEM((2, states, CHUNKS, inner), F32),
            pltpu.VMEM((cells, inner), F32),
            pltpu.VMEM((halves, cells, LANES), F32),
            pltpu.VMEM((4 * states, cells, LANES), F32),
        ],
        compiler_params=PARAMS,
        name="forward_scans",
    )
    axes = ("col", "row")
    lines = [exchange(embedded, "col"), exchange(turned, "row")]
    pairs = []
    for pair in range(2):
        two = slice(2 * pair, 2 * pair + 2)
        weights = (
            gain,
            value_weight,
            scan_weight[:, 2 * pair * group : 2 * (pair + 1) * group],
            step_weight[two],
            step_bias[two],
            decay_log[two],
        )
        pairs.append((weights, skip_gain[two]))
    kept, sums = ([], [])
    for pair in range(2):
        weights, skips = pairs[pair]
        outputs = forward(lines[pair], *weights, skips)
        kept.append(outputs[1:])
        sums.append(exchange(outputs[0], axes[pair]))

    firsts = pack_sizes(inner, width, rank, states)
    gate_rows = halves * width + inner + 8
    d_rows, d_cols, d_own, gate_packed = pl.pallas_call(
        functools.partial(gate_kernel, edge=edge),
        out_shape=(
            shape_of(cells, inner),
            shape_of(cells, inner),
            shape_of(cells, width),
            shape_of(gate_rows, LANES),
        ),
        scratch_shapes=[pltpu.VMEM((halves, cells, LANES), F32)],
        compiler_params=PARAMS,
        name="gate",
    )(
        embedded,
        gain,
        gate_weight,
        output_gain.reshape(1, inner),
        output_weight,
        cotangent.reshape(cells, width),
        sums[0],
        sums[1],
    )

    backward = pl.pallas_call(
        functools.partial(backward_kernel, rank=rank, states=states),
        out_shape=(shape_of(cells, width), shape_of(firsts[5], LANES)),
        scratch_shapes=[
            pltpu.VMEM((cells, inner), F32),
            pltpu.VMEM((2, states, CHUNKS, inner), F32),
            pltpu.VMEM((span + 1, states, CHUNKS, inner), F32),
            pltpu.VMEM((span, states, CHUNKS, inner), F32),
            pltpu.VMEM((cells, LANES), F32),
            pltpu.VMEM((cells, inner), F32),
            pltpu.VMEM((cells, inner), F32),
            pltpu.VMEM((states, CHUNKS, inner), F32),
            pltpu.VMEM((states, CHUNKS, inner), F32),
            pltpu.VMEM((halves, cells, LANES), F32),
            pltpu.VMEM((cells, inner), F32),
            pltpu.VMEM((4 * states, cells, LANES), F32),
            pltpu.VMEM((2 * states, cells, LANES), F32),
        ],
        compiler_params=PARAMS,
        name="backward_scans",
    )
    arriving = [exchange(d_rows, "col"), exchange(d_cols, "row")]
    outputs = []
    for pair in range(2):
        weights, skips = pairs[pair]
        outputs.append(backward(lines[pair], *weights, *kept[pair], arriving[pair], skips))
    returned = exchange(outputs[0][0], "col")

    row_count, col_count = (lax.axis_size("row"), lax.axis_size("col"))
    shared = firsts[1]
    stacked_rows = gate_rows + 2 * firsts[5] - shared
    stacked_rows += -stacked_rows % (row_count * 8)
    share_rows = stacked_rows // row_count
    blocks = pl.pallas_call(
        functools.partial(pack_kernel, shared=shared),
        out_shape=shape_of(row_count, edge + share_rows, LANES),
        scratch_shapes=[pltpu.VMEM((stacked_rows, LANES), F32)],
        compiler_params=PARAMS,
        name="pack",
    )(gate_packed, outputs[0][1], outputs[1][1], outputs[1][0])
    received = lax.all_to_all(blocks, "row", 0, 0)
    partial = jnp.sum(received[:, edge:], axis=0)
    partial = jnp.pad(partial, ((0, -share_rows % (col_count * 8)), (0, 0)))
    partial = partial.reshape(col_count, -1, LANES)
    owned = jnp.sum(lax.all_to_all(partial, "col", 0, 0), axis=0)
    column_sums = share(owned, "col").reshape(-1, LANES)[:share_rows]
    whole = share(column_sums, "row").reshape(stacked_rows, LANES)

    feature_grad = pl.pallas_call(
        functools.partial(finish_kernel, edge=edge),
        out_shape=shape_of(cells, width, dtype=BF16),
        scratch_shapes=[pltpu.VMEM((cells, width), F32)],
        compiler_params=PARAMS,
        name="finish",
    )(d_own, returned, received[:, :edge])
    grads = pl.pallas_call(
        functools.partial(unpack_kernel, scale=scale, rank=rank, states=states),
        out_shape=(
            shape_of(width, 2 * inner),
            shape_of(inner, 4 * group),
            shape_of(4, rank, inner),
            shape_of(4, inner),
            shape_of(4, states, inner),
            shape_of(4, inner),
            shape_of(1, width),
            shape_of(1, inner),
            shape_of(inner, width),
        ),
        compiler_params=PARAMS,
        name="unpack",
    )(whole)
    return (
        feature_grad.reshape(edge, across, width),
        *grads[:6],
        grads[6].reshape(width),
        grads[7].reshape(inner),
        grads[8],
    )


def solution(mesh):
    tiled = P("row", "col", None)
    in_specs = (P("row", "col"), tiled, tiled) + (P(),) * 10
    out_specs = (tiled,) + (P(),) * 9
    return jax.shard_map(local, mesh=mesh, in_specs=in_specs, out_specs=out_specs, check_vma=False)
```

```python
import functools

import jax
import jax.numpy as jnp
from jax import lax
from jax.experimental import pallas as pl
from jax.experimental.pallas import tpu as pltpu
from jax.sharding import PartitionSpec as P

EPS = 1e-05
HIGHEST = lax.Precision.HIGHEST
LOG2E = 1.4426950408889634
LN2 = 0.6931471805599453
CHUNKS = 8
LANES = 128
F32 = jnp.float32
BF16 = jnp.bfloat16
SMALL = pltpu.CompilerParams(vmem_limit_bytes=12 * 1024 * 1024)
MIDDLE = pltpu.CompilerParams(vmem_limit_bytes=20 * 1024 * 1024)
LARGE = pltpu.CompilerParams(vmem_limit_bytes=36 * 1024 * 1024)


def normalise(rows):
    average = jnp.mean(rows, axis=-1, keepdims=True)
    centred = rows - average
    spread = jnp.mean(centred * centred, axis=-1, keepdims=True)
    inverse = lax.rsqrt(spread + EPS)
    return centred * inverse, inverse


def normalise_pull(upstream, unit, inverse):
    first = jnp.mean(upstream, axis=-1, keepdims=True)
    second = jnp.mean(upstream * unit, axis=-1, keepdims=True)
    return inverse * (upstream - first - unit * second)


def sigmoid(before):
    return 1.0 / (1.0 + jnp.exp(-before))


def softplus(before):
    return jnp.maximum(before, 0.0) + jnp.log1p(jnp.exp(-jnp.abs(before)))


def product(left, right, over=((1,), (0,)), precision=None):
    return lax.dot_general(left, right, (over, ((), ())), precision=precision, preferred_element_type=F32)


def embed_kernel(classes, features, table, embedded, turned, *, edge):
    labels = lax.broadcasted_iota(jnp.int32, (classes.shape[0], table.shape[0]), 1)
    onehot = (classes[...] == labels).astype(F32)
    cells = features[...].astype(F32) + product(onehot, table[...], precision=HIGHEST)
    embedded[...] = cells
    for row in range(edge):
        turned[pl.ds(row, edge, stride=edge), :] = cells[row * edge : (row + 1) * edge]


def chain_chunks(total, state, upward):
    place = lax.broadcasted_iota(jnp.int32, state.shape, 0)
    reach = 1
    while reach < CHUNKS:
        shift = reach if upward else CHUNKS - reach
        inside = place >= reach if upward else place < CHUNKS - reach
        state = state + total * jnp.where(inside, pltpu.roll(state, shift, 0), 0.0)
        total = total * jnp.where(inside, pltpu.roll(total, shift, 0), 1.0)
        reach *= 2
    shift = 1 if upward else CHUNKS - 1
    inside = place >= 1 if upward else place < CHUNKS - 1
    return jnp.where(inside, pltpu.roll(state, shift, 0), 0.0)


def spread_rates(decay_log, rates, pair):
    for direction in range(2):
        scaled = -jnp.exp(decay_log[2 * pair + direction]) * LOG2E
        for entry in range(scaled.shape[0]):
            rates[direction, entry] = jnp.broadcast_to(
                scaled[entry : entry + 1], (CHUNKS, scaled.shape[1])
            )


def put_halves(target, rows):
    for half in range(target.shape[0]):
        target[half] = rows[:, half * LANES : (half + 1) * LANES]


def take_halves(source):
    return jnp.concatenate([source[half] for half in range(source.shape[0])], axis=1)


def load_interleaved(source):
    span = source.shape[0] // CHUNKS
    return jnp.concatenate(
        [source[pl.ds(place, CHUNKS, stride=span), :] for place in range(span)], axis=0
    )


def store_natural(target, rows):
    span = rows.shape[0] // CHUNKS
    for place in range(span):
        target[pl.ds(place, CHUNKS, stride=span), :] = rows[place * CHUNKS : (place + 1) * CHUNKS]


def sweep(span, advance, carried, unroll):
    def several(turn, state):
        for part in range(unroll):
            state = advance(turn * unroll + part, state)
        return state

    return lax.fori_loop(0, span // unroll, several, carried)


def expand_columns(flat, columns, rank, group):
    length, width = flat.shape
    wanted = group - rank
    padded = jnp.concatenate([flat, jnp.zeros((length, LANES - width), F32)], axis=1)
    high = padded.astype(BF16)
    low = (padded - high.astype(F32)).astype(BF16)
    both = jnp.concatenate([high, low], axis=1)
    row = lax.broadcasted_iota(jnp.int32, (2 * LANES, 2 * LANES), 0)
    lane = lax.broadcasted_iota(jnp.int32, (2 * LANES, 2 * LANES), 1)
    odd_lane = (lane >= LANES).astype(jnp.int32)
    copies = (row % 2 == odd_lane).astype(F32).astype(BF16)
    place = lax.broadcasted_iota(jnp.int32, (1, 2 * LANES), 1) % LANES // 2
    for direction in range(2):

        def one(pair, unused, direction=direction):
            chosen = (place == (direction * group + rank) // 2 + pair).astype(F32).astype(BF16)
            wide = product(both * chosen, copies)
            columns[direction * wanted + 2 * pair] = wide[:, :LANES]
            columns[direction * wanted + 2 * pair + 1] = wide[:, LANES:]
            return unused

        sweep(wanted // 2, one, 0, 8)


def sum_columns(terms, target, first):
    row = lax.broadcasted_iota(jnp.int32, (2 * LANES, LANES), 0)
    lane = lax.broadcasted_iota(jnp.int32, (2 * LANES, LANES), 1)
    copies = (lane % 2 == (row >= LANES).astype(jnp.int32)).astype(F32).astype(BF16)
    place = lax.broadcasted_iota(jnp.int32, target.shape, 1) // 2

    def one(pair, unused):
        both = jnp.concatenate([terms[2 * pair], terms[2 * pair + 1]], axis=1).astype(BF16)
        target[...] = jnp.where(place == first // 2 + pair, product(both, copies), target[...])
        return unused

    sweep(terms.shape[0] // 2, one, 0, 4)


def slot(place):
    return pl.ds(pl.multiple_of(place * CHUNKS, CHUNKS), CHUNKS)


def pair_sum(gains, pair):
    return gains[2 * pair : 2 * pair + 1] + gains[2 * pair + 1 : 2 * pair + 2]


def line_inputs(
    embedded,
    norm_gain,
    in_weight,
    scan_weight,
    step_weight,
    step_bias,
    targets,
    pair,
    rank,
    group,
):
    steps, values, columns = targets
    inner = values.shape[1]
    unit, inverse = normalise(load_interleaved(embedded))
    normed = (unit * norm_gain[...]).astype(BF16)
    mixed = product(normed, in_weight[:, :inner])
    sigma = sigmoid(mixed)
    rounded = (mixed * sigma).astype(BF16)
    flat = product(rounded, pair_rows(scan_weight, pair, group), ((1,), (1,)))
    expand_columns(flat, columns, rank, group)
    values[...] = rounded.astype(F32)
    lowranks, before = ([], [])
    for direction in range(2):
        index = 2 * pair + direction
        lowrank = flat[:, direction * group : direction * group + rank]
        lowranks.append(lowrank)
        before.append(
            product(lowrank, step_weight[index], precision=HIGHEST) + step_bias[index : index + 1]
        )
        steps[direction] = softplus(before[direction])
    return unit, inverse, normed, mixed, sigma, rounded, lowranks, before


def pair_rows(scan_weight, pair, group):
    return scan_weight[2 * pair * group : 2 * (pair + 1) * group]


def forward_kernel(
    embedded,
    norm_gain,
    in_weight,
    scan_weight,
    step_weight,
    step_bias,
    decay_log,
    skip_gain,
    result,
    starts,
    steps,
    values,
    rates,
    totals,
    natural,
    columns,
    *,
    pair,
    rank,
    states,
):
    length, inner = result.shape
    halves = inner // LANES
    span = length // CHUNKS
    group = rank + 2 * states
    unused = line_inputs(
        embedded,
        norm_gain,
        in_weight,
        scan_weight,
        step_weight,
        step_bias,
        (steps, values, columns),
        pair,
        rank,
        group,
    )
    totals[...] = values[...] * pair_sum(skip_gain, pair)
    spread_rates(decay_log, rates, pair)
    zero = jnp.zeros((CHUNKS, LANES), F32)

    for direction in range(2):
        source = direction * 2 * states
        probe = source + states

        def rows(turn, direction=direction):
            return slot(turn if direction == 0 else span - 1 - turn)

        for half in range(halves):
            lanes = slice(half * LANES, (half + 1) * LANES)

            def ending(turn, carried, direction=direction, lanes=lanes, rows=rows, source=source):
                state, total = carried
                at = rows(turn)
                step = steps[direction, at, lanes]
                drive = step * values[at, lanes]
                state = tuple(
                    jnp.exp2(step * rates[direction, n, :, lanes]) * state[n]
                    + columns[source + n, at, :] * drive
                    for n in range(states)
                )
                return (state, total + step)

            state, total = sweep(span, ending, ((zero,) * states, zero), 8)
            begin = []
            for n in range(states):
                factor = jnp.exp2(total * rates[direction, n, :, lanes])
                start = chain_chunks(factor, state[n], direction == 0)
                starts[direction, n, :, lanes] = start
                begin.append(start)

            def advance(
                turn, state, direction=direction, lanes=lanes, rows=rows, source=source, probe=probe
            ):
                at = rows(turn)
                step = steps[direction, at, lanes]
                drive = step * values[at, lanes]
                output = totals[at, lanes]
                after = []
                for n in range(states):
                    here = (
                        jnp.exp2(step * rates[direction, n, :, lanes]) * state[n]
                        + columns[source + n, at, :] * drive
                    )
                    output = output + columns[probe + n, at, :] * here
                    after.append(here)
                totals[at, lanes] = output
                return tuple(after)

            sweep(span, advance, tuple(begin), 8)
    for half in range(halves):
        store_natural(natural.at[half], totals[:, half * LANES : (half + 1) * LANES])
    result[...] = take_halves(natural)


def pack_sizes(inner, width, rank, states):
    halves = inner // LANES
    group = rank + 2 * states
    sizes = (halves * width, halves * 2 * group, halves * 2 * rank, halves * 2 * states, 8)
    firsts = [sum(sizes[:index]) for index in range(len(sizes) + 1)]
    return firsts


def pack_halves(target, first, rows):
    height, width = rows.shape
    for half in range(width // LANES):
        target[first + half * height : first + (half + 1) * height] = rows[
            :, half * LANES : (half + 1) * LANES
        ]


def gate_kernel(
    embedded,
    norm_gain,
    in_weight,
    output_gain,
    output_weight,
    cotangent,
    along_rows,
    along_cols,
    d_rows,
    d_cols,
    d_embedded,
    packed,
    turned,
    *,
    edge,
):
    inner, width = output_weight.shape
    halves = inner // LANES
    put_halves(turned, along_cols[...])
    total = along_rows[...] + jnp.concatenate(
        [
            jnp.concatenate(
                [turned[half, pl.ds(row, edge, stride=edge), :] for row in range(edge)], axis=0
            )
            for half in range(halves)
        ],
        axis=1,
    )
    base, inverse = normalise(embedded[...])
    gain = norm_gain[...]
    normed = (base * gain).astype(BF16)
    gate_weight = in_weight[:, inner:]
    gate_in = product(normed, gate_weight)
    sigma = sigmoid(gate_in)
    gate = gate_in * sigma
    slope = sigma * (1.0 + gate_in * (1.0 - sigma))
    unit, spread = normalise(total)
    strength = output_gain[...]
    gated = (unit * strength * gate).astype(BF16)
    upstream = cotangent[...]
    d_gated = product(upstream, output_weight[...], ((1,), (1,)))
    d_scaled = d_gated * gate
    d_total = normalise_pull(d_scaled * strength, unit, spread)
    d_rows[...] = d_total
    for half in range(halves):
        lanes = slice(half * LANES, (half + 1) * LANES)
        for row in range(edge):
            turned[half, pl.ds(row, edge, stride=edge), :] = d_total[
                row * edge : (row + 1) * edge, lanes
            ]
    d_cols[...] = take_halves(turned)
    d_gate = (d_gated * unit * strength * slope).astype(BF16)
    d_normed = product(d_gate, gate_weight, ((1,), (1,)))
    d_embedded[...] = normalise_pull(d_normed * gain, base, inverse) + upstream.astype(F32)
    first = halves * width
    pack_halves(packed, 0, product(normed, d_gate, ((0,), (0,))))
    packed[first : first + inner] = product(gated, upstream, ((0,), (0,)))
    last = first + inner
    packed[last : last + 8] = jnp.zeros((8, LANES), F32)
    packed[last : last + 1] = jnp.sum(d_normed * base, axis=0, keepdims=True)
    pack_halves(packed, last + 1, jnp.sum(d_scaled * unit, axis=0, keepdims=True))


def backward_kernel(
    embedded,
    norm_gain,
    in_weight,
    scan_weight,
    step_weight,
    step_bias,
    decay_log,
    skip_gain,
    starts,
    upstream,
    d_embedded,
    packed,
    steps,
    values,
    rates,
    history,
    decays,
    d_projected,
    d_values,
    d_steps,
    d_rates,
    enter,
    natural,
    arriving_lines,
    columns,
    terms,
    slopes,
    *,
    pair,
    rank,
    states,
):
    length, inner = upstream.shape
    width = embedded.shape[1]
    halves = inner // LANES
    span = length // CHUNKS
    group = rank + 2 * states
    firsts = pack_sizes(inner, width, rank, states)
    gain = norm_gain[...]
    unit, inverse, normed, mixed, sigma, rounded, lowranks, before = line_inputs(
        embedded,
        norm_gain,
        in_weight,
        scan_weight,
        step_weight,
        step_bias,
        (steps, values, columns),
        pair,
        rank,
        group,
    )
    for direction in range(2):
        slopes[direction] = sigmoid(before[direction])
    put_halves(natural, upstream[...])
    incoming = jnp.concatenate(
        [load_interleaved(natural.at[half]) for half in range(halves)], axis=1
    )
    arriving_lines[...] = incoming
    d_values[...] = incoming * pair_sum(skip_gain, pair)
    d_projected[...] = jnp.zeros(d_projected.shape, F32)
    spread_rates(decay_log, rates, pair)
    zero = jnp.zeros((CHUNKS, LANES), F32)
    packed[firsts[4] : firsts[5]] = jnp.zeros((8, LANES), F32)
    pack_halves(packed, firsts[4] + 1, jnp.sum(incoming * values[...], axis=0, keepdims=True))

    for direction in range(2):
        source = direction * 2 * states
        probe = source + states
        d_rates[...] = jnp.zeros(d_rates.shape, F32)

        def rows(turn, direction=direction):
            return slot(turn if direction == 0 else span - 1 - turn)

        for half in range(halves):
            lanes = slice(half * LANES, (half + 1) * LANES)

            def advance(turn, carried, direction=direction, lanes=lanes, rows=rows, source=source):
                state, total = carried
                at = rows(turn)
                step = steps[direction, at, lanes]
                drive = step * values[at, lanes]
                after = []
                for n in range(states):
                    decay = jnp.exp2(step * rates[direction, n, :, lanes])
                    decays[turn, n, :, lanes] = decay
                    here = decay * state[n] + columns[source + n, at, :] * drive
                    history[turn + 1, n, :, lanes] = here
                    after.append(here)
                return (tuple(after), total + step)

            begin = tuple(starts[direction, n, :, lanes] for n in range(states))
            for n in range(states):
                history[0, n, :, lanes] = begin[n]
            unused, total = sweep(span, advance, (begin, zero), 4)

            def retreat(turn, carried, lanes=lanes, rows=rows, probe=probe):
                back = span - 1 - turn
                at = rows(back)
                arriving = arriving_lines[at, lanes]
                return tuple(
                    decays[back, n, :, lanes]
                    * (columns[probe + n, at, :] * arriving + carried[n])
                    for n in range(states)
                )

            carried = sweep(span, retreat, (zero,) * states, 8)
            for n in range(states):
                factor = jnp.exp2(total * rates[direction, n, :, lanes])
                enter[n, :, lanes] = chain_chunks(factor, carried[n], direction == 1)

        def pull(turn, carried, direction=direction, rows=rows, source=source, probe=probe):
            back = span - 1 - turn
            at = rows(back)
            step = steps[direction, at, :]
            value = values[at, :]
            drive = step * value
            arriving = arriving_lines[at, :]
            d_drive = jnp.zeros((CHUNKS, inner), F32)
            d_step = jnp.zeros((CHUNKS, inner), F32)
            after = []
            for n in range(states):
                reader = jnp.concatenate([columns[probe + n, at, :]] * halves, axis=1)
                writer = jnp.concatenate([columns[source + n, at, :]] * halves, axis=1)
                adjoint = reader * arriving + carried[n]
                leaving = decays[back, n] * adjoint
                after.append(leaving)
                d_probe = arriving * history[back + 1, n]
                d_source = adjoint * drive
                terms[n, at, :] = sum(
                    d_source[:, half * LANES : (half + 1) * LANES] for half in range(halves)
                )
                terms[states + n, at, :] = sum(
                    d_probe[:, half * LANES : (half + 1) * LANES] for half in range(halves)
                )
                d_drive = d_drive + adjoint * writer
                weight = leaving * history[back, n]
                d_step = d_step + weight * rates[direction, n]
                d_rates[n] = d_rates[n] + weight * step
            d_values[at, :] = d_values[at, :] + step * d_drive
            d_steps[at, :] = value * d_drive + LN2 * d_step
            return tuple(after)

        sweep(span, pull, tuple(enter[n] for n in range(states)), 2)
        first = direction * group
        sum_columns(terms, d_projected, first + rank)
        pack_halves(
            packed,
            firsts[3] + direction * halves * states,
            jnp.sum(d_rates[...], axis=1) * -jnp.exp(decay_log[2 * pair + direction]),
        )
        d_before = d_steps[...] * slopes[direction]
        pack_halves(
            packed,
            firsts[4] + 1 + halves * (1 + direction),
            jnp.sum(d_before, axis=0, keepdims=True),
        )
        pack_halves(
            packed,
            firsts[2] + direction * halves * rank,
            product(lowranks[direction], d_before, ((0,), (0,)), HIGHEST),
        )
        d_projected[:, first : first + rank] = product(
            d_before, step_weight[2 * pair + direction], ((1,), (1,)), HIGHEST
        )

    d_flat = d_projected[:, : 2 * group].astype(BF16)
    pack_halves(packed, firsts[1], product(d_flat, rounded, ((0,), (0,))))
    d_all = product(d_flat, pair_rows(scan_weight, pair, group)) + d_values[...]
    d_mixed = (d_all * sigma * (1.0 + mixed * (1.0 - sigma))).astype(BF16)
    pack_halves(packed, 0, product(normed, d_mixed, ((0,), (0,))))
    d_normed = product(d_mixed, in_weight[:, :inner], ((1,), (1,)))
    packed[firsts[4] : firsts[4] + 1] = jnp.sum(d_normed * unit, axis=0, keepdims=True)
    store_natural(d_embedded, normalise_pull(d_normed * gain, unit, inverse))


def finish_kernel(own, along_rows, along_cols, gradient, turned, *, edge):
    turned[...] = along_cols[...].reshape(turned.shape)
    natural = jnp.concatenate(
        [turned[pl.ds(row, edge, stride=edge), :] for row in range(edge)], axis=0
    )
    gradient[...] = (own[...] + along_rows[...].reshape(own.shape) + natural).astype(BF16)


def pack_kernel(gate, first, second, lines, blocks, stacked, *, shared):
    count, height, unused = blocks.shape
    edge = lines.shape[0] // count
    gate_rows, scan_rows = (gate.shape[0], first.shape[0])
    rest = scan_rows - shared
    stacked[:gate_rows] = gate[...]
    stacked[gate_rows : gate_rows + shared] = first[:shared] + second[:shared]
    start = gate_rows + shared
    stacked[start : start + rest] = first[shared:]
    stacked[start + rest : start + 2 * rest] = second[shared:]
    start = start + 2 * rest
    stacked[start:] = jnp.zeros((stacked.shape[0] - start, LANES), F32)
    for block in range(count):
        blocks[block, :edge] = lines[block * edge : (block + 1) * edge]
        blocks[block, edge:] = stacked[block * (height - edge) : (block + 1) * (height - edge)]


def unpack_kernel(
    whole,
    in_weight,
    scan_weight,
    step_weight,
    step_bias,
    decay,
    skip,
    norm_gain,
    output_gain,
    output_weight,
    *,
    scale,
    rank,
    states,
):
    width, double = in_weight.shape
    inner = double // 2
    halves = inner // LANES
    group = rank + 2 * states
    firsts = pack_sizes(inner, width, rank, states)
    shared = firsts[1]

    def joined(start, height):
        return scale * jnp.concatenate(
            [whole[start + half * height : start + (half + 1) * height] for half in range(halves)],
            axis=1,
        )

    gate = halves * width + inner + 8
    in_weight[:, inner:] = joined(0, width)
    in_weight[:, :inner] = joined(gate, width)
    output_weight[...] = scale * whole[halves * width : halves * width + inner]
    small = halves * width + inner
    output_gain[...] = joined(small + 1, 1)
    gains = whole[small : small + 1]
    projected = []
    for pair in range(2):
        start = gate + shared + pair * (firsts[5] - shared) - shared
        projected.append(joined(start + firsts[1], 2 * group))
        for direction in range(2):
            index = 2 * pair + direction
            step_weight[index] = joined(start + firsts[2] + direction * halves * rank, rank)
            decay[index] = joined(start + firsts[3] + direction * halves * states, states)
            base = start + firsts[4] + 1
            skip[index : index + 1] = joined(base, 1)
            step_bias[index : index + 1] = joined(base + halves * (1 + direction), 1)
        gains = gains + whole[start + firsts[4] : start + firsts[4] + 1]
    norm_gain[...] = scale * gains
    scan_weight[...] = jnp.concatenate(projected, axis=0)


def shape_of(*sizes, dtype=F32):
    return jax.ShapeDtypeStruct(sizes, dtype)


def exchange(rows, axis):
    count = lax.axis_size(axis)
    length, width = rows.shape
    blocks = rows.reshape(count, length // count, width)
    return lax.all_to_all(blocks, axis, 0, 0).reshape(length, width)


def share(block, axis):
    count = lax.axis_size(axis)
    copies = jnp.broadcast_to(block[None], (count,) + block.shape)
    return lax.all_to_all(copies, axis, 0, 0)


def local(
    classes,
    features,
    cotangent,
    table,
    norm_gain,
    in_weight,
    scan_weight,
    step_weight,
    step_bias,
    decay_log,
    skip_gain,
    output_gain,
    output_weight,
):
    edge, across, width = features.shape
    inner = output_weight.shape[0]
    rank, states = (step_weight.shape[1], decay_log.shape[1])
    group = rank + 2 * states
    cells = edge * across
    span = cells // CHUNKS
    halves = inner // LANES
    scale = float(cells * lax.axis_size("row") * lax.axis_size("col")) ** (-0.5)
    gain = norm_gain.reshape(1, width)

    embedded, turned = pl.pallas_call(
        functools.partial(embed_kernel, edge=edge),
        out_shape=(shape_of(cells, width), shape_of(cells, width)),
        compiler_params=SMALL,
        name="embed",
    )(classes.reshape(cells, 1), features.reshape(cells, width), table)

    weights = (gain, in_weight, scan_weight.T, step_weight, step_bias, decay_log, skip_gain)

    def forward(pair, line):
        return pl.pallas_call(
            functools.partial(forward_kernel, pair=pair, rank=rank, states=states),
            out_shape=(shape_of(cells, inner), shape_of(2, states, CHUNKS, inner)),
            scratch_shapes=[
                pltpu.VMEM((2, cells, inner), F32),
                pltpu.VMEM((cells, inner), F32),
                pltpu.VMEM((2, states, CHUNKS, inner), F32),
                pltpu.VMEM((cells, inner), F32),
                pltpu.VMEM((halves, cells, LANES), F32),
                pltpu.VMEM((4 * states, cells, LANES), F32),
            ],
            compiler_params=MIDDLE,
            cost_estimate=pl.CostEstimate(
                flops=48 * 1024 * cells * inner,
                bytes_accessed=8 * cells * inner,
                transcendentals=4 * states * cells * inner,
            ),
            name="forward_scans",
        )(line, *weights)

    row_line, col_line = (exchange(embedded, "col"), exchange(turned, "row"))
    row_sums, row_starts = forward(0, row_line)
    row_sums, col_line = lax.optimization_barrier((row_sums, col_line))
    along_rows = exchange(row_sums, "col")
    col_sums, col_starts = forward(1, col_line)
    along_rows, col_sums = lax.optimization_barrier((along_rows, col_sums))
    along_cols = exchange(col_sums, "row")

    firsts = pack_sizes(inner, width, rank, states)
    gate_rows = halves * width + inner + 8
    d_rows, d_cols, d_own, gate_packed = pl.pallas_call(
        functools.partial(gate_kernel, edge=edge),
        out_shape=(
            shape_of(cells, inner),
            shape_of(cells, inner),
            shape_of(cells, width),
            shape_of(gate_rows, LANES),
        ),
        scratch_shapes=[pltpu.VMEM((halves, cells, LANES), F32)],
        compiler_params=SMALL,
        name="gate",
    )(
        embedded,
        gain,
        in_weight,
        output_gain.reshape(1, inner),
        output_weight,
        cotangent.reshape(cells, width),
        along_rows,
        along_cols,
    )

    def backward(pair, line, starts, arriving):
        return pl.pallas_call(
            functools.partial(backward_kernel, pair=pair, rank=rank, states=states),
            out_shape=(shape_of(cells, width), shape_of(firsts[5], LANES)),
            scratch_shapes=[
                pltpu.VMEM((2, cells, inner), F32),
                pltpu.VMEM((cells, inner), F32),
                pltpu.VMEM((2, states, CHUNKS, inner), F32),
                pltpu.VMEM((span + 1, states, CHUNKS, inner), F32),
                pltpu.VMEM((span, states, CHUNKS, inner), F32),
                pltpu.VMEM((cells, LANES), F32),
                pltpu.VMEM((cells, inner), F32),
                pltpu.VMEM((cells, inner), F32),
                pltpu.VMEM((states, CHUNKS, inner), F32),
                pltpu.VMEM((states, CHUNKS, inner), F32),
                pltpu.VMEM((halves, cells, LANES), F32),
                pltpu.VMEM((cells, inner), F32),
                pltpu.VMEM((4 * states, cells, LANES), F32),
                pltpu.VMEM((2 * states, cells, LANES), F32),
                pltpu.VMEM((2, cells, inner), F32),
            ],
            compiler_params=LARGE,
            cost_estimate=pl.CostEstimate(
                flops=96 * 1024 * cells * inner,
                bytes_accessed=8 * cells * inner,
                transcendentals=4 * states * cells * inner,
            ),
            name="backward_scans",
        )(line, *weights, starts, arriving)

    arriving_cols = exchange(d_cols, "row")
    arriving_rows = exchange(d_rows, "col")
    back_cols, packed_cols = backward(1, col_line, col_starts, arriving_cols)
    back_rows, packed_rows = backward(0, row_line, row_starts, arriving_rows)

    row_count, col_count = (lax.axis_size("row"), lax.axis_size("col"))
    shared = firsts[1]
    stacked_rows = gate_rows + 2 * firsts[5] - shared
    stacked_rows += -stacked_rows % (row_count * 8)
    share_rows = stacked_rows // row_count
    blocks = pl.pallas_call(
        functools.partial(pack_kernel, shared=shared),
        out_shape=shape_of(row_count, edge + share_rows, LANES),
        scratch_shapes=[pltpu.VMEM((stacked_rows, LANES), F32)],
        compiler_params=SMALL,
        name="pack",
    )(gate_packed, packed_rows, packed_cols, back_cols)
    received = lax.all_to_all(blocks, "row", 0, 0)
    partial = jnp.sum(received[:, edge:], axis=0)
    lines_back = back_rows.reshape(col_count, cells // col_count, width)
    copies = jnp.broadcast_to(partial[None], (col_count,) + partial.shape)
    crossed = lax.all_to_all(jnp.concatenate([lines_back, copies], axis=1), "col", 0, 0)
    column_sums = jnp.sum(crossed[:, across:], axis=0)
    whole = share(column_sums, "row").reshape(stacked_rows, LANES)

    feature_grad = pl.pallas_call(
        functools.partial(finish_kernel, edge=edge),
        out_shape=shape_of(cells, width, dtype=BF16),
        scratch_shapes=[pltpu.VMEM((cells, width), F32)],
        compiler_params=SMALL,
        name="finish",
    )(d_own, crossed[:, :across], received[:, :edge])
    grads = pl.pallas_call(
        functools.partial(unpack_kernel, scale=scale, rank=rank, states=states),
        out_shape=(
            shape_of(width, 2 * inner),
            shape_of(4 * group, inner),
            shape_of(4, rank, inner),
            shape_of(4, inner),
            shape_of(4, states, inner),
            shape_of(4, inner),
            shape_of(1, width),
            shape_of(1, inner),
            shape_of(inner, width),
        ),
        compiler_params=SMALL,
        name="unpack",
    )(whole)
    return (
        feature_grad.reshape(edge, across, width),
        grads[0],
        grads[1].T,
        *grads[2:6],
        grads[6].reshape(width),
        grads[7].reshape(inner),
        grads[8],
    )


def solution(mesh):
    tiled = P("row", "col", None)
    in_specs = (P("row", "col"), tiled, tiled) + (P(),) * 10
    out_specs = (tiled,) + (P(),) * 9
    return jax.shard_map(local, mesh=mesh, in_specs=in_specs, out_specs=out_specs, check_vma=False)
```

```python
import functools

import jax
import jax.numpy as jnp
from jax import lax
from jax.experimental import pallas as pl
from jax.experimental.pallas import tpu as pltpu
from jax.sharding import PartitionSpec as P

EPS = 1e-05
HIGHEST = lax.Precision.HIGHEST
LOG2E = 1.4426950408889634
LN2 = 0.6931471805599453
CHUNKS = 8
LANES = 128
F32 = jnp.float32
BF16 = jnp.bfloat16
SMALL = pltpu.CompilerParams(vmem_limit_bytes=12 * 1024 * 1024)
MIDDLE = pltpu.CompilerParams(vmem_limit_bytes=20 * 1024 * 1024)
LARGE = pltpu.CompilerParams(vmem_limit_bytes=36 * 1024 * 1024)


def normalise(rows):
    average = jnp.mean(rows, axis=-1, keepdims=True)
    centred = rows - average
    spread = jnp.mean(centred * centred, axis=-1, keepdims=True)
    inverse = lax.rsqrt(spread + EPS)
    return centred * inverse, inverse


def normalise_pull(upstream, unit, inverse):
    first = jnp.mean(upstream, axis=-1, keepdims=True)
    second = jnp.mean(upstream * unit, axis=-1, keepdims=True)
    return inverse * (upstream - first - unit * second)


def sigmoid(before):
    return 1.0 / (1.0 + jnp.exp(-before))


def softplus(before):
    return jnp.maximum(before, 0.0) + jnp.log1p(jnp.exp(-jnp.abs(before)))


def product(left, right, over=((1,), (0,)), precision=None):
    return lax.dot_general(left, right, (over, ((), ())), precision=precision, preferred_element_type=F32)


def embed_kernel(classes, features, table, embedded, turned, *, edge):
    labels = lax.broadcasted_iota(jnp.int32, (classes.shape[0], table.shape[0]), 1)
    onehot = (classes[...] == labels).astype(F32)
    cells = features[...].astype(F32) + product(onehot, table[...], precision=HIGHEST)
    embedded[...] = cells
    for row in range(edge):
        turned[pl.ds(row, edge, stride=edge), :] = cells[row * edge : (row + 1) * edge]


def chain_chunks(total, state, upward):
    place = lax.broadcasted_iota(jnp.int32, state.shape, 0)
    reach = 1
    while reach < CHUNKS:
        shift = reach if upward else CHUNKS - reach
        inside = place >= reach if upward else place < CHUNKS - reach
        state = state + total * jnp.where(inside, pltpu.roll(state, shift, 0), 0.0)
        total = total * jnp.where(inside, pltpu.roll(total, shift, 0), 1.0)
        reach *= 2
    shift = 1 if upward else CHUNKS - 1
    inside = place >= 1 if upward else place < CHUNKS - 1
    return jnp.where(inside, pltpu.roll(state, shift, 0), 0.0)


def spread_rates(decay_log, rates, pair):
    for direction in range(2):
        scaled = -jnp.exp(decay_log[2 * pair + direction]) * LOG2E
        for entry in range(scaled.shape[0]):
            rates[direction, entry] = jnp.broadcast_to(
                scaled[entry : entry + 1], (CHUNKS, scaled.shape[1])
            )


def put_halves(target, rows):
    for half in range(target.shape[0]):
        target[half] = rows[:, half * LANES : (half + 1) * LANES]


def take_halves(source):
    return jnp.concatenate([source[half] for half in range(source.shape[0])], axis=1)


def load_interleaved(source):
    span = source.shape[0] // CHUNKS
    return jnp.concatenate(
        [source[pl.ds(place, CHUNKS, stride=span), :] for place in range(span)], axis=0
    )


def store_natural(target, rows):
    span = rows.shape[0] // CHUNKS
    for place in range(span):
        target[pl.ds(place, CHUNKS, stride=span), :] = rows[place * CHUNKS : (place + 1) * CHUNKS]


def sweep(span, advance, carried, unroll):
    def several(turn, state):
        for part in range(unroll):
            state = advance(turn * unroll + part, state)
        return state

    return lax.fori_loop(0, span // unroll, several, carried)


def expand_columns(flat, columns, rank, group):
    length, width = flat.shape
    wanted = group - rank
    padded = jnp.concatenate([flat, jnp.zeros((length, LANES - width), F32)], axis=1)
    high = padded.astype(BF16)
    low = (padded - high.astype(F32)).astype(BF16)
    both = jnp.concatenate([high, low], axis=1)
    row = lax.broadcasted_iota(jnp.int32, (2 * LANES, 2 * LANES), 0)
    lane = lax.broadcasted_iota(jnp.int32, (2 * LANES, 2 * LANES), 1)
    odd_lane = (lane >= LANES).astype(jnp.int32)
    copies = (row % 2 == odd_lane).astype(F32).astype(BF16)
    place = lax.broadcasted_iota(jnp.int32, (1, 2 * LANES), 1) % LANES // 2
    for direction in range(2):

        def one(pair, unused, direction=direction):
            chosen = (place == (direction * group + rank) // 2 + pair).astype(F32).astype(BF16)
            wide = product(both * chosen, copies)
            columns[direction * wanted + 2 * pair] = wide[:, :LANES]
            columns[direction * wanted + 2 * pair + 1] = wide[:, LANES:]
            return unused

        sweep(wanted // 2, one, 0, 16)


def sum_columns(terms, target, first):
    row = lax.broadcasted_iota(jnp.int32, (2 * LANES, LANES), 0)
    lane = lax.broadcasted_iota(jnp.int32, (2 * LANES, LANES), 1)
    copies = (lane % 2 == (row >= LANES).astype(jnp.int32)).astype(F32).astype(BF16)
    place = lax.broadcasted_iota(jnp.int32, target.shape, 1) // 2

    def one(pair, unused):
        both = jnp.concatenate([terms[2 * pair], terms[2 * pair + 1]], axis=1).astype(BF16)
        target[...] = jnp.where(place == first // 2 + pair, product(both, copies), target[...])
        return unused

    sweep(terms.shape[0] // 2, one, 0, 16)


def slot(place):
    return pl.ds(pl.multiple_of(place * CHUNKS, CHUNKS), CHUNKS)


def pair_sum(gains, pair):
    return gains[2 * pair : 2 * pair + 1] + gains[2 * pair + 1 : 2 * pair + 2]


def line_inputs(
    embedded,
    norm_gain,
    in_weight,
    scan_weight,
    step_weight,
    step_bias,
    targets,
    pair,
    rank,
    group,
):
    steps, values, columns = targets
    inner = values.shape[1]
    unit, inverse = normalise(load_interleaved(embedded))
    normed = (unit * norm_gain[...]).astype(BF16)
    mixed = product(normed, in_weight[:, :inner])
    sigma = sigmoid(mixed)
    rounded = (mixed * sigma).astype(BF16)
    flat = product(rounded, pair_rows(scan_weight, pair, group), ((1,), (1,)))
    expand_columns(flat, columns, rank, group)
    values[...] = rounded.astype(F32)
    lowranks, before = ([], [])
    for direction in range(2):
        index = 2 * pair + direction
        lowrank = flat[:, direction * group : direction * group + rank]
        lowranks.append(lowrank)
        before.append(
            product(lowrank, step_weight[index], precision=HIGHEST) + step_bias[index : index + 1]
        )
        steps[direction] = softplus(before[direction])
    return unit, inverse, normed, mixed, sigma, rounded, lowranks, before


def pair_rows(scan_weight, pair, group):
    return scan_weight[2 * pair * group : 2 * (pair + 1) * group]


def forward_kernel(
    embedded,
    norm_gain,
    in_weight,
    scan_weight,
    step_weight,
    step_bias,
    decay_log,
    skip_gain,
    result,
    starts,
    steps,
    values,
    rates,
    totals,
    natural,
    columns,
    *,
    pair,
    rank,
    states,
):
    length, inner = result.shape
    halves = inner // LANES
    span = length // CHUNKS
    group = rank + 2 * states
    unused = line_inputs(
        embedded,
        norm_gain,
        in_weight,
        scan_weight,
        step_weight,
        step_bias,
        (steps, values, columns),
        pair,
        rank,
        group,
    )
    totals[...] = values[...] * pair_sum(skip_gain, pair)
    spread_rates(decay_log, rates, pair)
    zero = jnp.zeros((CHUNKS, LANES), F32)

    for direction in range(2):
        source = direction * 2 * states
        probe = source + states

        def rows(turn, direction=direction):
            return slot(turn if direction == 0 else span - 1 - turn)

        for half in range(halves):
            lanes = slice(half * LANES, (half + 1) * LANES)

            def ending(turn, carried, direction=direction, lanes=lanes, rows=rows, source=source):
                state, total = carried
                at = rows(turn)
                step = steps[direction, at, lanes]
                drive = step * values[at, lanes]
                state = tuple(
                    jnp.exp2(step * rates[direction, n, :, lanes]) * state[n]
                    + columns[source + n, at, :] * drive
                    for n in range(states)
                )
                return (state, total + step)

            state, total = sweep(span, ending, ((zero,) * states, zero), 8)
            begin = []
            for n in range(states):
                factor = jnp.exp2(total * rates[direction, n, :, lanes])
                start = chain_chunks(factor, state[n], direction == 0)
                starts[direction, n, :, lanes] = start
                begin.append(start)

            def advance(
                turn, state, direction=direction, lanes=lanes, rows=rows, source=source, probe=probe
            ):
                at = rows(turn)
                step = steps[direction, at, lanes]
                drive = step * values[at, lanes]
                output = totals[at, lanes]
                after = []
                for n in range(states):
                    here = (
                        jnp.exp2(step * rates[direction, n, :, lanes]) * state[n]
                        + columns[source + n, at, :] * drive
                    )
                    output = output + columns[probe + n, at, :] * here
                    after.append(here)
                totals[at, lanes] = output
                return tuple(after)

            sweep(span, advance, tuple(begin), 8)
    for half in range(halves):
        store_natural(natural.at[half], totals[:, half * LANES : (half + 1) * LANES])
    result[...] = take_halves(natural)


def pack_sizes(inner, width, rank, states):
    halves = inner // LANES
    group = rank + 2 * states
    sizes = (halves * width, halves * 2 * group, halves * 2 * rank, halves * 2 * states, 8)
    firsts = [sum(sizes[:index]) for index in range(len(sizes) + 1)]
    return firsts


def pack_halves(target, first, rows):
    height, width = rows.shape
    for half in range(width // LANES):
        target[first + half * height : first + (half + 1) * height] = rows[
            :, half * LANES : (half + 1) * LANES
        ]


def gate_kernel(
    embedded,
    norm_gain,
    in_weight,
    output_gain,
    output_weight,
    cotangent,
    along_rows,
    along_cols,
    d_rows,
    d_cols,
    d_embedded,
    packed,
    turned,
    *,
    edge,
):
    inner, width = output_weight.shape
    halves = inner // LANES
    put_halves(turned, along_cols[...])
    total = along_rows[...] + jnp.concatenate(
        [
            jnp.concatenate(
                [turned[half, pl.ds(row, edge, stride=edge), :] for row in range(edge)], axis=0
            )
            for half in range(halves)
        ],
        axis=1,
    )
    base, inverse = normalise(embedded[...])
    gain = norm_gain[...]
    normed = (base * gain).astype(BF16)
    gate_weight = in_weight[:, inner:]
    gate_in = product(normed, gate_weight)
    sigma = sigmoid(gate_in)
    gate = gate_in * sigma
    slope = sigma * (1.0 + gate_in * (1.0 - sigma))
    unit, spread = normalise(total)
    strength = output_gain[...]
    gated = (unit * strength * gate).astype(BF16)
    upstream = cotangent[...]
    d_gated = product(upstream, output_weight[...], ((1,), (1,)))
    d_scaled = d_gated * gate
    d_total = normalise_pull(d_scaled * strength, unit, spread)
    d_rows[...] = d_total
    for half in range(halves):
        lanes = slice(half * LANES, (half + 1) * LANES)
        for row in range(edge):
            turned[half, pl.ds(row, edge, stride=edge), :] = d_total[
                row * edge : (row + 1) * edge, lanes
            ]
    d_cols[...] = take_halves(turned)
    d_gate = (d_gated * unit * strength * slope).astype(BF16)
    d_normed = product(d_gate, gate_weight, ((1,), (1,)))
    d_embedded[...] = normalise_pull(d_normed * gain, base, inverse) + upstream.astype(F32)
    first = halves * width
    pack_halves(packed, 0, product(normed, d_gate, ((0,), (0,))))
    packed[first : first + inner] = product(gated, upstream, ((0,), (0,)))
    last = first + inner
    packed[last : last + 8] = jnp.zeros((8, LANES), F32)
    packed[last : last + 1] = jnp.sum(d_normed * base, axis=0, keepdims=True)
    pack_halves(packed, last + 1, jnp.sum(d_scaled * unit, axis=0, keepdims=True))


def backward_kernel(
    embedded,
    norm_gain,
    in_weight,
    scan_weight,
    step_weight,
    step_bias,
    decay_log,
    skip_gain,
    starts,
    upstream,
    d_embedded,
    packed,
    steps,
    values,
    rates,
    history,
    decays,
    d_projected,
    d_values,
    d_steps,
    d_rates,
    enter,
    natural,
    arriving_lines,
    columns,
    terms,
    slopes,
    *,
    pair,
    rank,
    states,
):
    length, inner = upstream.shape
    width = embedded.shape[1]
    halves = inner // LANES
    span = length // CHUNKS
    group = rank + 2 * states
    firsts = pack_sizes(inner, width, rank, states)
    gain = norm_gain[...]
    unit, inverse, normed, mixed, sigma, rounded, lowranks, before = line_inputs(
        embedded,
        norm_gain,
        in_weight,
        scan_weight,
        step_weight,
        step_bias,
        (steps, values, columns),
        pair,
        rank,
        group,
    )
    for direction in range(2):
        slopes[direction] = sigmoid(before[direction])
    put_halves(natural, upstream[...])
    incoming = jnp.concatenate(
        [load_interleaved(natural.at[half]) for half in range(halves)], axis=1
    )
    arriving_lines[...] = incoming
    d_values[...] = incoming * pair_sum(skip_gain, pair)
    d_projected[...] = jnp.zeros(d_projected.shape, F32)
    spread_rates(decay_log, rates, pair)
    zero = jnp.zeros((CHUNKS, LANES), F32)
    packed[firsts[4] : firsts[5]] = jnp.zeros((8, LANES), F32)
    pack_halves(packed, firsts[4] + 1, jnp.sum(incoming * values[...], axis=0, keepdims=True))

    for direction in range(2):
        source = direction * 2 * states
        probe = source + states
        d_rates[...] = jnp.zeros(d_rates.shape, F32)

        def rows(turn, direction=direction):
            return slot(turn if direction == 0 else span - 1 - turn)

        for half in range(halves):
            lanes = slice(half * LANES, (half + 1) * LANES)

            def advance(turn, carried, direction=direction, lanes=lanes, rows=rows, source=source):
                state, total = carried
                at = rows(turn)
                step = steps[direction, at, lanes]
                drive = step * values[at, lanes]
                after = []
                for n in range(states):
                    decay = jnp.exp2(step * rates[direction, n, :, lanes])
                    decays[turn, n, :, lanes] = decay
                    here = decay * state[n] + columns[source + n, at, :] * drive
                    history[turn + 1, n, :, lanes] = here
                    after.append(here)
                return (tuple(after), total + step)

            begin = tuple(starts[direction, n, :, lanes] for n in range(states))
            for n in range(states):
                history[0, n, :, lanes] = begin[n]
            unused, total = sweep(span, advance, (begin, zero), 4)

            def retreat(turn, carried, lanes=lanes, rows=rows, probe=probe):
                back = span - 1 - turn
                at = rows(back)
                arriving = arriving_lines[at, lanes]
                return tuple(
                    decays[back, n, :, lanes]
                    * (columns[probe + n, at, :] * arriving + carried[n])
                    for n in range(states)
                )

            carried = sweep(span, retreat, (zero,) * states, 8)
            for n in range(states):
                factor = jnp.exp2(total * rates[direction, n, :, lanes])
                enter[n, :, lanes] = chain_chunks(factor, carried[n], direction == 1)

        def pull(turn, carried, direction=direction, rows=rows, source=source, probe=probe):
            back = span - 1 - turn
            at = rows(back)
            step = steps[direction, at, :]
            value = values[at, :]
            drive = step * value
            arriving = arriving_lines[at, :]
            d_drive = jnp.zeros((CHUNKS, inner), F32)
            d_step = jnp.zeros((CHUNKS, inner), F32)
            after = []
            for n in range(states):
                reader = jnp.concatenate([columns[probe + n, at, :]] * halves, axis=1)
                writer = jnp.concatenate([columns[source + n, at, :]] * halves, axis=1)
                adjoint = reader * arriving + carried[n]
                leaving = decays[back, n] * adjoint
                after.append(leaving)
                d_probe = arriving * history[back + 1, n]
                d_source = adjoint * drive
                terms[n, at, :] = sum(
                    d_source[:, half * LANES : (half + 1) * LANES] for half in range(halves)
                )
                terms[states + n, at, :] = sum(
                    d_probe[:, half * LANES : (half + 1) * LANES] for half in range(halves)
                )
                d_drive = d_drive + adjoint * writer
                weight = leaving * history[back, n]
                d_step = d_step + weight * rates[direction, n]
                d_rates[n] = d_rates[n] + weight * step
            d_values[at, :] = d_values[at, :] + step * d_drive
            d_steps[at, :] = value * d_drive + LN2 * d_step
            return tuple(after)

        sweep(span, pull, tuple(enter[n] for n in range(states)), 4)
        first = direction * group
        sum_columns(terms, d_projected, first + rank)
        pack_halves(
            packed,
            firsts[3] + direction * halves * states,
            jnp.sum(d_rates[...], axis=1) * -jnp.exp(decay_log[2 * pair + direction]),
        )
        d_before = d_steps[...] * slopes[direction]
        pack_halves(
            packed,
            firsts[4] + 1 + halves * (1 + direction),
            jnp.sum(d_before, axis=0, keepdims=True),
        )
        pack_halves(
            packed,
            firsts[2] + direction * halves * rank,
            product(lowranks[direction], d_before, ((0,), (0,)), HIGHEST),
        )
        d_projected[:, first : first + rank] = product(
            d_before, step_weight[2 * pair + direction], ((1,), (1,)), HIGHEST
        )

    d_flat = d_projected[:, : 2 * group].astype(BF16)
    pack_halves(packed, firsts[1], product(d_flat, rounded, ((0,), (0,))))
    d_all = product(d_flat, pair_rows(scan_weight, pair, group)) + d_values[...]
    d_mixed = (d_all * sigma * (1.0 + mixed * (1.0 - sigma))).astype(BF16)
    pack_halves(packed, 0, product(normed, d_mixed, ((0,), (0,))))
    d_normed = product(d_mixed, in_weight[:, :inner], ((1,), (1,)))
    packed[firsts[4] : firsts[4] + 1] = jnp.sum(d_normed * unit, axis=0, keepdims=True)
    store_natural(d_embedded, normalise_pull(d_normed * gain, unit, inverse))


def finish_kernel(own, along_rows, along_cols, gradient, turned, *, edge):
    turned[...] = along_cols[...].reshape(turned.shape)
    natural = jnp.concatenate(
        [turned[pl.ds(row, edge, stride=edge), :] for row in range(edge)], axis=0
    )
    gradient[...] = (own[...] + along_rows[...].reshape(own.shape) + natural).astype(BF16)


def pack_kernel(gate, first, second, lines, blocks, stacked, *, shared):
    count, height, unused = blocks.shape
    edge = lines.shape[0] // count
    gate_rows, scan_rows = (gate.shape[0], first.shape[0])
    rest = scan_rows - shared
    stacked[:gate_rows] = gate[...]
    stacked[gate_rows : gate_rows + shared] = first[:shared] + second[:shared]
    start = gate_rows + shared
    stacked[start : start + rest] = first[shared:]
    stacked[start + rest : start + 2 * rest] = second[shared:]
    start = start + 2 * rest
    stacked[start:] = jnp.zeros((stacked.shape[0] - start, LANES), F32)
    for block in range(count):
        blocks[block, :edge] = lines[block * edge : (block + 1) * edge]
        blocks[block, edge:] = stacked[block * (height - edge) : (block + 1) * (height - edge)]


def unpack_kernel(
    whole,
    in_weight,
    scan_weight,
    step_weight,
    step_bias,
    decay,
    skip,
    norm_gain,
    output_gain,
    output_weight,
    *,
    scale,
    rank,
    states,
):
    width, double = in_weight.shape
    inner = double // 2
    halves = inner // LANES
    group = rank + 2 * states
    firsts = pack_sizes(inner, width, rank, states)
    shared = firsts[1]

    def joined(start, height):
        return scale * jnp.concatenate(
            [whole[start + half * height : start + (half + 1) * height] for half in range(halves)],
            axis=1,
        )

    gate = halves * width + inner + 8
    in_weight[:, inner:] = joined(0, width)
    in_weight[:, :inner] = joined(gate, width)
    output_weight[...] = scale * whole[halves * width : halves * width + inner]
    small = halves * width + inner
    output_gain[...] = joined(small + 1, 1)
    gains = whole[small : small + 1]
    projected = []
    for pair in range(2):
        start = gate + shared + pair * (firsts[5] - shared) - shared
        projected.append(joined(start + firsts[1], 2 * group))
        for direction in range(2):
            index = 2 * pair + direction
            step_weight[index] = joined(start + firsts[2] + direction * halves * rank, rank)
            decay[index] = joined(start + firsts[3] + direction * halves * states, states)
            base = start + firsts[4] + 1
            skip[index : index + 1] = joined(base, 1)
            step_bias[index : index + 1] = joined(base + halves * (1 + direction), 1)
        gains = gains + whole[start + firsts[4] : start + firsts[4] + 1]
    norm_gain[...] = scale * gains
    scan_weight[...] = jnp.concatenate(projected, axis=0)


def shape_of(*sizes, dtype=F32):
    return jax.ShapeDtypeStruct(sizes, dtype)


def exchange(rows, axis):
    count = lax.axis_size(axis)
    length, width = rows.shape
    blocks = rows.reshape(count, length // count, width)
    return lax.all_to_all(blocks, axis, 0, 0).reshape(length, width)


def share(block, axis):
    count = lax.axis_size(axis)
    copies = jnp.broadcast_to(block[None], (count,) + block.shape)
    return lax.all_to_all(copies, axis, 0, 0)


def local(
    classes,
    features,
    cotangent,
    table,
    norm_gain,
    in_weight,
    scan_weight,
    step_weight,
    step_bias,
    decay_log,
    skip_gain,
    output_gain,
    output_weight,
):
    edge, across, width = features.shape
    inner = output_weight.shape[0]
    rank, states = (step_weight.shape[1], decay_log.shape[1])
    group = rank + 2 * states
    cells = edge * across
    span = cells // CHUNKS
    halves = inner // LANES
    scale = float(cells * lax.axis_size("row") * lax.axis_size("col")) ** (-0.5)
    gain = norm_gain.reshape(1, width)

    embedded, turned = pl.pallas_call(
        functools.partial(embed_kernel, edge=edge),
        out_shape=(shape_of(cells, width), shape_of(cells, width)),
        compiler_params=SMALL,
        name="embed",
    )(classes.reshape(cells, 1), features.reshape(cells, width), table)

    weights = (gain, in_weight, scan_weight.T, step_weight, step_bias, decay_log, skip_gain)

    def forward(pair, line):
        return pl.pallas_call(
            functools.partial(forward_kernel, pair=pair, rank=rank, states=states),
            out_shape=(shape_of(cells, inner), shape_of(2, states, CHUNKS, inner)),
            scratch_shapes=[
                pltpu.VMEM((2, cells, inner), F32),
                pltpu.VMEM((cells, inner), F32),
                pltpu.VMEM((2, states, CHUNKS, inner), F32),
                pltpu.VMEM((cells, inner), F32),
                pltpu.VMEM((halves, cells, LANES), F32),
                pltpu.VMEM((4 * states, cells, LANES), F32),
            ],
            compiler_params=MIDDLE,
            cost_estimate=pl.CostEstimate(
                flops=48 * 1024 * cells * inner,
                bytes_accessed=8 * cells * inner,
                transcendentals=4 * states * cells * inner,
            ),
            name="forward_scans",
        )(line, *weights)

    row_line, col_line = (exchange(embedded, "col"), exchange(turned, "row"))
    row_sums, row_starts = forward(0, row_line)
    row_sums, col_line = lax.optimization_barrier((row_sums, col_line))
    along_rows = exchange(row_sums, "col")
    col_sums, col_starts = forward(1, col_line)
    along_rows, col_sums = lax.optimization_barrier((along_rows, col_sums))
    along_cols = exchange(col_sums, "row")

    firsts = pack_sizes(inner, width, rank, states)
    gate_rows = halves * width + inner + 8
    d_rows, d_cols, d_own, gate_packed = pl.pallas_call(
        functools.partial(gate_kernel, edge=edge),
        out_shape=(
            shape_of(cells, inner),
            shape_of(cells, inner),
            shape_of(cells, width),
            shape_of(gate_rows, LANES),
        ),
        scratch_shapes=[pltpu.VMEM((halves, cells, LANES), F32)],
        compiler_params=SMALL,
        name="gate",
    )(
        embedded,
        gain,
        in_weight,
        output_gain.reshape(1, inner),
        output_weight,
        cotangent.reshape(cells, width),
        along_rows,
        along_cols,
    )

    def backward(pair, line, starts, arriving):
        return pl.pallas_call(
            functools.partial(backward_kernel, pair=pair, rank=rank, states=states),
            out_shape=(shape_of(cells, width), shape_of(firsts[5], LANES)),
            scratch_shapes=[
                pltpu.VMEM((2, cells, inner), F32),
                pltpu.VMEM((cells, inner), F32),
                pltpu.VMEM((2, states, CHUNKS, inner), F32),
                pltpu.VMEM((span + 1, states, CHUNKS, inner), F32),
                pltpu.VMEM((span, states, CHUNKS, inner), F32),
                pltpu.VMEM((cells, LANES), F32),
                pltpu.VMEM((cells, inner), F32),
                pltpu.VMEM((cells, inner), F32),
                pltpu.VMEM((states, CHUNKS, inner), F32),
                pltpu.VMEM((states, CHUNKS, inner), F32),
                pltpu.VMEM((halves, cells, LANES), F32),
                pltpu.VMEM((cells, inner), F32),
                pltpu.VMEM((4 * states, cells, LANES), F32),
                pltpu.VMEM((2 * states, cells, LANES), F32),
                pltpu.VMEM((2, cells, inner), F32),
            ],
            compiler_params=LARGE,
            cost_estimate=pl.CostEstimate(
                flops=96 * 1024 * cells * inner,
                bytes_accessed=8 * cells * inner,
                transcendentals=4 * states * cells * inner,
            ),
            name="backward_scans",
        )(line, *weights, starts, arriving)

    arriving_cols = exchange(d_cols, "row")
    arriving_rows = exchange(d_rows, "col")
    back_cols, packed_cols = backward(1, col_line, col_starts, arriving_cols)
    back_rows, packed_rows = backward(0, row_line, row_starts, arriving_rows)

    row_count, col_count = (lax.axis_size("row"), lax.axis_size("col"))
    shared = firsts[1]
    stacked_rows = gate_rows + 2 * firsts[5] - shared
    stacked_rows += -stacked_rows % (row_count * 8)
    share_rows = stacked_rows // row_count
    blocks = pl.pallas_call(
        functools.partial(pack_kernel, shared=shared),
        out_shape=shape_of(row_count, edge + share_rows, LANES),
        scratch_shapes=[pltpu.VMEM((stacked_rows, LANES), F32)],
        compiler_params=SMALL,
        name="pack",
    )(gate_packed, packed_rows, packed_cols, back_cols)
    received = lax.all_to_all(blocks, "row", 0, 0)
    partial = jnp.sum(received[:, edge:], axis=0)
    lines_back = back_rows.reshape(col_count, cells // col_count, width)
    copies = jnp.broadcast_to(partial[None], (col_count,) + partial.shape)
    crossed = lax.all_to_all(jnp.concatenate([lines_back, copies], axis=1), "col", 0, 0)
    column_sums = jnp.sum(crossed[:, across:], axis=0)
    whole = share(column_sums, "row").reshape(stacked_rows, LANES)

    feature_grad = pl.pallas_call(
        functools.partial(finish_kernel, edge=edge),
        out_shape=shape_of(cells, width, dtype=BF16),
        scratch_shapes=[pltpu.VMEM((cells, width), F32)],
        compiler_params=SMALL,
        name="finish",
    )(d_own, crossed[:, :across], received[:, :edge])
    grads = pl.pallas_call(
        functools.partial(unpack_kernel, scale=scale, rank=rank, states=states),
        out_shape=(
            shape_of(width, 2 * inner),
            shape_of(4 * group, inner),
            shape_of(4, rank, inner),
            shape_of(4, inner),
            shape_of(4, states, inner),
            shape_of(4, inner),
            shape_of(1, width),
            shape_of(1, inner),
            shape_of(inner, width),
        ),
        compiler_params=SMALL,
        name="unpack",
    )(whole)
    return (
        feature_grad.reshape(edge, across, width),
        grads[0],
        grads[1].T,
        *grads[2:6],
        grads[6].reshape(width),
        grads[7].reshape(inner),
        grads[8],
    )


def solution(mesh):
    tiled = P("row", "col", None)
    in_specs = (P("row", "col"), tiled, tiled) + (P(),) * 10
    out_specs = (tiled,) + (P(),) * 9
    return jax.shard_map(local, mesh=mesh, in_specs=in_specs, out_specs=out_specs, check_vma=False)
```

```python
import functools

import jax
import jax.numpy as jnp
from jax import lax
from jax.experimental import pallas as pl
from jax.experimental.pallas import tpu as pltpu
from jax.sharding import PartitionSpec as P

EPS = 1e-05
HIGHEST = lax.Precision.HIGHEST
LOG2E = 1.4426950408889634
LN2 = 0.6931471805599453
CHUNKS = 8
LANES = 128
F32 = jnp.float32
BF16 = jnp.bfloat16
SMALL = pltpu.CompilerParams(vmem_limit_bytes=12 * 1024 * 1024)
MIDDLE = pltpu.CompilerParams(vmem_limit_bytes=20 * 1024 * 1024)
LARGE = pltpu.CompilerParams(vmem_limit_bytes=36 * 1024 * 1024)


def normalise(rows):
    average = jnp.mean(rows, axis=-1, keepdims=True)
    centred = rows - average
    spread = jnp.mean(centred * centred, axis=-1, keepdims=True)
    inverse = lax.rsqrt(spread + EPS)
    return centred * inverse, inverse


def normalise_pull(upstream, unit, inverse):
    first = jnp.mean(upstream, axis=-1, keepdims=True)
    second = jnp.mean(upstream * unit, axis=-1, keepdims=True)
    return inverse * (upstream - first - unit * second)


def sigmoid(before):
    return 1.0 / (1.0 + jnp.exp(-before))


def softplus(before):
    return jnp.maximum(before, 0.0) + jnp.log1p(jnp.exp(-jnp.abs(before)))


def product(left, right, over=((1,), (0,)), precision=None):
    return lax.dot_general(left, right, (over, ((), ())), precision=precision, preferred_element_type=F32)


def embed_kernel(classes, features, table, embedded, turned, *, edge):
    labels = lax.broadcasted_iota(jnp.int32, (classes.shape[0], table.shape[0]), 1)
    onehot = (classes[...] == labels).astype(F32)
    cells = features[...].astype(F32) + product(onehot, table[...], precision=HIGHEST)
    embedded[...] = cells
    for row in range(edge):
        turned[pl.ds(row, edge, stride=edge), :] = cells[row * edge : (row + 1) * edge]


def chain_chunks(total, state, upward):
    place = lax.broadcasted_iota(jnp.int32, state.shape, 0)
    reach = 1
    while reach < CHUNKS:
        shift = reach if upward else CHUNKS - reach
        inside = place >= reach if upward else place < CHUNKS - reach
        state = state + total * jnp.where(inside, pltpu.roll(state, shift, 0), 0.0)
        total = total * jnp.where(inside, pltpu.roll(total, shift, 0), 1.0)
        reach *= 2
    shift = 1 if upward else CHUNKS - 1
    inside = place >= 1 if upward else place < CHUNKS - 1
    return jnp.where(inside, pltpu.roll(state, shift, 0), 0.0)


def spread_rates(decay_log, rates, pair):
    for direction in range(2):
        scaled = -jnp.exp(decay_log[2 * pair + direction]) * LOG2E
        for entry in range(scaled.shape[0]):
            rates[direction, entry] = jnp.broadcast_to(
                scaled[entry : entry + 1], (CHUNKS, scaled.shape[1])
            )


def put_halves(target, rows):
    for half in range(target.shape[0]):
        target[half] = rows[:, half * LANES : (half + 1) * LANES]


def take_halves(source):
    return jnp.concatenate([source[half] for half in range(source.shape[0])], axis=1)


def load_interleaved(source):
    span = source.shape[0] // CHUNKS
    return jnp.concatenate(
        [source[pl.ds(place, CHUNKS, stride=span), :] for place in range(span)], axis=0
    )


def store_natural(target, rows):
    span = rows.shape[0] // CHUNKS
    for place in range(span):
        target[pl.ds(place, CHUNKS, stride=span), :] = rows[place * CHUNKS : (place + 1) * CHUNKS]


def sweep(span, advance, carried, unroll):
    def several(turn, state):
        for part in range(unroll):
            state = advance(turn * unroll + part, state)
        return state

    return lax.fori_loop(0, span // unroll, several, carried)


def expand_columns(flat, columns, rank, group):
    length, width = flat.shape
    wanted = group - rank
    padded = jnp.concatenate([flat, jnp.zeros((length, LANES - width), F32)], axis=1)
    high = padded.astype(BF16)
    low = (padded - high.astype(F32)).astype(BF16)
    both = jnp.concatenate([high, low], axis=1)
    row = lax.broadcasted_iota(jnp.int32, (2 * LANES, 2 * LANES), 0)
    lane = lax.broadcasted_iota(jnp.int32, (2 * LANES, 2 * LANES), 1)
    odd_lane = (lane >= LANES).astype(jnp.int32)
    copies = (row % 2 == odd_lane).astype(F32).astype(BF16)
    place = lax.broadcasted_iota(jnp.int32, (1, 2 * LANES), 1) % LANES // 2
    for direction in range(2):

        def one(pair, unused, direction=direction):
            chosen = (place == (direction * group + rank) // 2 + pair).astype(F32).astype(BF16)
            wide = product(both * chosen, copies)
            columns[direction * wanted + 2 * pair] = wide[:, :LANES]
            columns[direction * wanted + 2 * pair + 1] = wide[:, LANES:]
            return unused

        sweep(wanted // 2, one, 0, 16)


def sum_columns(terms, target, first):
    row = lax.broadcasted_iota(jnp.int32, (2 * LANES, LANES), 0)
    lane = lax.broadcasted_iota(jnp.int32, (2 * LANES, LANES), 1)
    copies = (lane % 2 == (row >= LANES).astype(jnp.int32)).astype(F32).astype(BF16)
    place = lax.broadcasted_iota(jnp.int32, target.shape, 1) // 2

    def one(pair, unused):
        both = jnp.concatenate([terms[2 * pair], terms[2 * pair + 1]], axis=1).astype(BF16)
        target[...] = jnp.where(place == first // 2 + pair, product(both, copies), target[...])
        return unused

    sweep(terms.shape[0] // 2, one, 0, 16)


def slot(place):
    return pl.ds(pl.multiple_of(place * CHUNKS, CHUNKS), CHUNKS)


def pair_sum(gains, pair):
    return gains[2 * pair : 2 * pair + 1] + gains[2 * pair + 1 : 2 * pair + 2]


def line_inputs(
    embedded,
    norm_gain,
    in_weight,
    scan_weight,
    step_weight,
    step_bias,
    targets,
    pair,
    rank,
    group,
):
    steps, values, columns = targets
    inner = values.shape[1]
    unit, inverse = normalise(load_interleaved(embedded))
    normed = (unit * norm_gain[...]).astype(BF16)
    mixed = product(normed, in_weight[:, :inner])
    sigma = sigmoid(mixed)
    rounded = (mixed * sigma).astype(BF16)
    flat = product(rounded, pair_rows(scan_weight, pair, group), ((1,), (1,)))
    expand_columns(flat, columns, rank, group)
    values[...] = rounded.astype(F32)
    lowranks, before = ([], [])
    for direction in range(2):
        index = 2 * pair + direction
        lowrank = flat[:, direction * group : direction * group + rank]
        lowranks.append(lowrank)
        before.append(
            product(lowrank, step_weight[index], precision=HIGHEST) + step_bias[index : index + 1]
        )
        steps[direction] = softplus(before[direction])
    return unit, inverse, normed, mixed, sigma, rounded, lowranks, before


def pair_rows(scan_weight, pair, group):
    return scan_weight[2 * pair * group : 2 * (pair + 1) * group]


def forward_kernel(
    embedded,
    norm_gain,
    in_weight,
    scan_weight,
    step_weight,
    step_bias,
    decay_log,
    skip_gain,
    result,
    starts,
    steps,
    values,
    rates,
    totals,
    natural,
    columns,
    *,
    pair,
    rank,
    states,
):
    length, inner = result.shape
    halves = inner // LANES
    span = length // CHUNKS
    group = rank + 2 * states
    unused = line_inputs(
        embedded,
        norm_gain,
        in_weight,
        scan_weight,
        step_weight,
        step_bias,
        (steps, values, columns),
        pair,
        rank,
        group,
    )
    totals[...] = values[...] * pair_sum(skip_gain, pair)
    spread_rates(decay_log, rates, pair)
    zero = jnp.zeros((CHUNKS, LANES), F32)

    for direction in range(2):
        source = direction * 2 * states
        probe = source + states

        def rows(turn, direction=direction):
            return slot(turn if direction == 0 else span - 1 - turn)

        for half in range(halves):
            lanes = slice(half * LANES, (half + 1) * LANES)

            def ending(turn, carried, direction=direction, lanes=lanes, rows=rows, source=source):
                state, total = carried
                at = rows(turn)
                step = steps[direction, at, lanes]
                drive = step * values[at, lanes]
                state = tuple(
                    jnp.exp2(step * rates[direction, n, :, lanes]) * state[n]
                    + columns[source + n, at, :] * drive
                    for n in range(states)
                )
                return (state, total + step)

            state, total = sweep(span, ending, ((zero,) * states, zero), 8)
            begin = []
            for n in range(states):
                factor = jnp.exp2(total * rates[direction, n, :, lanes])
                start = chain_chunks(factor, state[n], direction == 0)
                starts[direction, n, :, lanes] = start
                begin.append(start)

            def advance(
                turn, state, direction=direction, lanes=lanes, rows=rows, source=source, probe=probe
            ):
                at = rows(turn)
                step = steps[direction, at, lanes]
                drive = step * values[at, lanes]
                output = totals[at, lanes]
                after = []
                for n in range(states):
                    here = (
                        jnp.exp2(step * rates[direction, n, :, lanes]) * state[n]
                        + columns[source + n, at, :] * drive
                    )
                    output = output + columns[probe + n, at, :] * here
                    after.append(here)
                totals[at, lanes] = output
                return tuple(after)

            sweep(span, advance, tuple(begin), 8)
    for half in range(halves):
        store_natural(natural.at[half], totals[:, half * LANES : (half + 1) * LANES])
    result[...] = take_halves(natural)


def pack_sizes(inner, width, rank, states):
    halves = inner // LANES
    group = rank + 2 * states
    sizes = (halves * width, halves * 2 * group, halves * 2 * rank, halves * 2 * states, 8)
    firsts = [sum(sizes[:index]) for index in range(len(sizes) + 1)]
    return firsts


def pack_halves(target, first, rows):
    height, width = rows.shape
    for half in range(width // LANES):
        target[first + half * height : first + (half + 1) * height] = rows[
            :, half * LANES : (half + 1) * LANES
        ]


def gate_kernel(
    embedded,
    norm_gain,
    in_weight,
    output_gain,
    output_weight,
    cotangent,
    along_rows,
    along_cols,
    d_rows,
    d_cols,
    d_embedded,
    packed,
    turned,
    *,
    edge,
):
    inner, width = output_weight.shape
    halves = inner // LANES
    put_halves(turned, along_cols[...])
    total = along_rows[...] + jnp.concatenate(
        [
            jnp.concatenate(
                [turned[half, pl.ds(row, edge, stride=edge), :] for row in range(edge)], axis=0
            )
            for half in range(halves)
        ],
        axis=1,
    )
    base, inverse = normalise(embedded[...])
    gain = norm_gain[...]
    normed = (base * gain).astype(BF16)
    gate_weight = in_weight[:, inner:]
    gate_in = product(normed, gate_weight)
    sigma = sigmoid(gate_in)
    gate = gate_in * sigma
    slope = sigma * (1.0 + gate_in * (1.0 - sigma))
    unit, spread = normalise(total)
    strength = output_gain[...]
    gated = (unit * strength * gate).astype(BF16)
    upstream = cotangent[...]
    d_gated = product(upstream, output_weight[...], ((1,), (1,)))
    d_scaled = d_gated * gate
    d_total = normalise_pull(d_scaled * strength, unit, spread)
    d_rows[...] = d_total
    for half in range(halves):
        lanes = slice(half * LANES, (half + 1) * LANES)
        for row in range(edge):
            turned[half, pl.ds(row, edge, stride=edge), :] = d_total[
                row * edge : (row + 1) * edge, lanes
            ]
    d_cols[...] = take_halves(turned)
    d_gate = (d_gated * unit * strength * slope).astype(BF16)
    d_normed = product(d_gate, gate_weight, ((1,), (1,)))
    d_embedded[...] = normalise_pull(d_normed * gain, base, inverse) + upstream.astype(F32)
    first = halves * width
    pack_halves(packed, 0, product(normed, d_gate, ((0,), (0,))))
    packed[first : first + inner] = product(gated, upstream, ((0,), (0,)))
    last = first + inner
    packed[last : last + 8] = jnp.zeros((8, LANES), F32)
    packed[last : last + 1] = jnp.sum(d_normed * base, axis=0, keepdims=True)
    pack_halves(packed, last + 1, jnp.sum(d_scaled * unit, axis=0, keepdims=True))


def backward_kernel(
    embedded,
    norm_gain,
    in_weight,
    scan_weight,
    step_weight,
    step_bias,
    decay_log,
    skip_gain,
    starts,
    upstream,
    d_embedded,
    packed,
    steps,
    values,
    rates,
    history,
    decays,
    d_projected,
    d_values,
    d_steps,
    d_rates,
    enter,
    natural,
    arriving_lines,
    columns,
    terms,
    slopes,
    *,
    pair,
    rank,
    states,
):
    length, inner = upstream.shape
    width = embedded.shape[1]
    halves = inner // LANES
    span = length // CHUNKS
    group = rank + 2 * states
    firsts = pack_sizes(inner, width, rank, states)
    gain = norm_gain[...]
    unit, inverse, normed, mixed, sigma, rounded, lowranks, before = line_inputs(
        embedded,
        norm_gain,
        in_weight,
        scan_weight,
        step_weight,
        step_bias,
        (steps, values, columns),
        pair,
        rank,
        group,
    )
    for direction in range(2):
        slopes[direction] = sigmoid(before[direction])
    put_halves(natural, upstream[...])
    incoming = jnp.concatenate(
        [load_interleaved(natural.at[half]) for half in range(halves)], axis=1
    )
    arriving_lines[...] = incoming
    d_values[...] = incoming * pair_sum(skip_gain, pair)
    d_projected[...] = jnp.zeros(d_projected.shape, F32)
    spread_rates(decay_log, rates, pair)
    zero = jnp.zeros((CHUNKS, LANES), F32)
    packed[firsts[4] : firsts[5]] = jnp.zeros((8, LANES), F32)
    pack_halves(packed, firsts[4] + 1, jnp.sum(incoming * values[...], axis=0, keepdims=True))

    for direction in range(2):
        source = direction * 2 * states
        probe = source + states
        d_rates[...] = jnp.zeros(d_rates.shape, F32)

        def rows(turn, direction=direction):
            return slot(turn if direction == 0 else span - 1 - turn)

        for half in range(halves):
            lanes = slice(half * LANES, (half + 1) * LANES)

            def advance(turn, carried, direction=direction, lanes=lanes, rows=rows, source=source):
                state, total = carried
                at = rows(turn)
                step = steps[direction, at, lanes]
                drive = step * values[at, lanes]
                after = []
                for n in range(states):
                    decay = jnp.exp2(step * rates[direction, n, :, lanes])
                    decays[turn, n, :, lanes] = decay
                    here = decay * state[n] + columns[source + n, at, :] * drive
                    history[turn + 1, n, :, lanes] = here
                    after.append(here)
                return (tuple(after), total + step)

            begin = tuple(starts[direction, n, :, lanes] for n in range(states))
            for n in range(states):
                history[0, n, :, lanes] = begin[n]
            unused, total = sweep(span, advance, (begin, zero), 8)

            def retreat(turn, carried, lanes=lanes, rows=rows, probe=probe):
                back = span - 1 - turn
                at = rows(back)
                arriving = arriving_lines[at, lanes]
                return tuple(
                    decays[back, n, :, lanes]
                    * (columns[probe + n, at, :] * arriving + carried[n])
                    for n in range(states)
                )

            carried = sweep(span, retreat, (zero,) * states, 16)
            for n in range(states):
                factor = jnp.exp2(total * rates[direction, n, :, lanes])
                enter[n, :, lanes] = chain_chunks(factor, carried[n], direction == 1)

        def pull(turn, carried, direction=direction, rows=rows, source=source, probe=probe):
            back = span - 1 - turn
            at = rows(back)
            step = steps[direction, at, :]
            value = values[at, :]
            drive = step * value
            arriving = arriving_lines[at, :]
            d_drive = jnp.zeros((CHUNKS, inner), F32)
            d_step = jnp.zeros((CHUNKS, inner), F32)
            after = []
            for n in range(states):
                reader = jnp.concatenate([columns[probe + n, at, :]] * halves, axis=1)
                writer = jnp.concatenate([columns[source + n, at, :]] * halves, axis=1)
                adjoint = reader * arriving + carried[n]
                leaving = decays[back, n] * adjoint
                after.append(leaving)
                d_probe = arriving * history[back + 1, n]
                d_source = adjoint * drive
                terms[n, at, :] = sum(
                    d_source[:, half * LANES : (half + 1) * LANES] for half in range(halves)
                )
                terms[states + n, at, :] = sum(
                    d_probe[:, half * LANES : (half + 1) * LANES] for half in range(halves)
                )
                d_drive = d_drive + adjoint * writer
                weight = leaving * history[back, n]
                d_step = d_step + weight * rates[direction, n]
                d_rates[n] = d_rates[n] + weight * step
            d_values[at, :] = d_values[at, :] + step * d_drive
            d_steps[at, :] = value * d_drive + LN2 * d_step
            return tuple(after)

        sweep(span, pull, tuple(enter[n] for n in range(states)), 4)
        first = direction * group
        sum_columns(terms, d_projected, first + rank)
        pack_halves(
            packed,
            firsts[3] + direction * halves * states,
            jnp.sum(d_rates[...], axis=1) * -jnp.exp(decay_log[2 * pair + direction]),
        )
        d_before = d_steps[...] * slopes[direction]
        pack_halves(
            packed,
            firsts[4] + 1 + halves * (1 + direction),
            jnp.sum(d_before, axis=0, keepdims=True),
        )
        pack_halves(
            packed,
            firsts[2] + direction * halves * rank,
            product(lowranks[direction], d_before, ((0,), (0,)), HIGHEST),
        )
        d_projected[:, first : first + rank] = product(
            d_before, step_weight[2 * pair + direction], ((1,), (1,))
        )

    d_flat = d_projected[:, : 2 * group].astype(BF16)
    pack_halves(packed, firsts[1], product(d_flat, rounded, ((0,), (0,))))
    d_all = product(d_flat, pair_rows(scan_weight, pair, group)) + d_values[...]
    d_mixed = (d_all * sigma * (1.0 + mixed * (1.0 - sigma))).astype(BF16)
    pack_halves(packed, 0, product(normed, d_mixed, ((0,), (0,))))
    d_normed = product(d_mixed, in_weight[:, :inner], ((1,), (1,)))
    packed[firsts[4] : firsts[4] + 1] = jnp.sum(d_normed * unit, axis=0, keepdims=True)
    store_natural(d_embedded, normalise_pull(d_normed * gain, unit, inverse))


def finish_kernel(own, along_rows, along_cols, gradient, turned, *, edge):
    turned[...] = along_cols[...].reshape(turned.shape)
    natural = jnp.concatenate(
        [turned[pl.ds(row, edge, stride=edge), :] for row in range(edge)], axis=0
    )
    gradient[...] = (own[...] + along_rows[...].reshape(own.shape) + natural).astype(BF16)


def pack_kernel(gate, first, second, lines, blocks, stacked, *, shared):
    count, height, unused = blocks.shape
    edge = lines.shape[0] // count
    gate_rows, scan_rows = (gate.shape[0], first.shape[0])
    rest = scan_rows - shared
    stacked[:gate_rows] = gate[...]
    stacked[gate_rows : gate_rows + shared] = first[:shared] + second[:shared]
    start = gate_rows + shared
    stacked[start : start + rest] = first[shared:]
    stacked[start + rest : start + 2 * rest] = second[shared:]
    start = start + 2 * rest
    stacked[start:] = jnp.zeros((stacked.shape[0] - start, LANES), F32)
    for block in range(count):
        blocks[block, :edge] = lines[block * edge : (block + 1) * edge]
        blocks[block, edge:] = stacked[block * (height - edge) : (block + 1) * (height - edge)]


def unpack_kernel(
    whole,
    in_weight,
    scan_weight,
    step_weight,
    step_bias,
    decay,
    skip,
    norm_gain,
    output_gain,
    output_weight,
    *,
    scale,
    rank,
    states,
):
    width, double = in_weight.shape
    inner = double // 2
    halves = inner // LANES
    group = rank + 2 * states
    firsts = pack_sizes(inner, width, rank, states)
    shared = firsts[1]

    def joined(start, height):
        return scale * jnp.concatenate(
            [whole[start + half * height : start + (half + 1) * height] for half in range(halves)],
            axis=1,
        )

    gate = halves * width + inner + 8
    in_weight[:, inner:] = joined(0, width)
    in_weight[:, :inner] = joined(gate, width)
    output_weight[...] = scale * whole[halves * width : halves * width + inner]
    small = halves * width + inner
    output_gain[...] = joined(small + 1, 1)
    gains = whole[small : small + 1]
    projected = []
    for pair in range(2):
        start = gate + shared + pair * (firsts[5] - shared) - shared
        projected.append(joined(start + firsts[1], 2 * group))
        for direction in range(2):
            index = 2 * pair + direction
            step_weight[index] = joined(start + firsts[2] + direction * halves * rank, rank)
            decay[index] = joined(start + firsts[3] + direction * halves * states, states)
            base = start + firsts[4] + 1
            skip[index : index + 1] = joined(base, 1)
            step_bias[index : index + 1] = joined(base + halves * (1 + direction), 1)
        gains = gains + whole[start + firsts[4] : start + firsts[4] + 1]
    norm_gain[...] = scale * gains
    scan_weight[...] = jnp.concatenate(projected, axis=0)


def shape_of(*sizes, dtype=F32):
    return jax.ShapeDtypeStruct(sizes, dtype)


def exchange(rows, axis):
    count = lax.axis_size(axis)
    length, width = rows.shape
    blocks = rows.reshape(count, length // count, width)
    return lax.all_to_all(blocks, axis, 0, 0).reshape(length, width)


def share(block, axis):
    count = lax.axis_size(axis)
    copies = jnp.broadcast_to(block[None], (count,) + block.shape)
    return lax.all_to_all(copies, axis, 0, 0)


def local(
    classes,
    features,
    cotangent,
    table,
    norm_gain,
    in_weight,
    scan_weight,
    step_weight,
    step_bias,
    decay_log,
    skip_gain,
    output_gain,
    output_weight,
):
    edge, across, width = features.shape
    inner = output_weight.shape[0]
    rank, states = (step_weight.shape[1], decay_log.shape[1])
    group = rank + 2 * states
    cells = edge * across
    span = cells // CHUNKS
    halves = inner // LANES
    scale = float(cells * lax.axis_size("row") * lax.axis_size("col")) ** (-0.5)
    gain = norm_gain.reshape(1, width)

    embedded, turned = pl.pallas_call(
        functools.partial(embed_kernel, edge=edge),
        out_shape=(shape_of(cells, width), shape_of(cells, width)),
        compiler_params=SMALL,
        name="embed",
    )(classes.reshape(cells, 1), features.reshape(cells, width), table)

    weights = (gain, in_weight, scan_weight.T, step_weight, step_bias, decay_log, skip_gain)

    def forward(pair, line):
        return pl.pallas_call(
            functools.partial(forward_kernel, pair=pair, rank=rank, states=states),
            out_shape=(shape_of(cells, inner), shape_of(2, states, CHUNKS, inner)),
            scratch_shapes=[
                pltpu.VMEM((2, cells, inner), F32),
                pltpu.VMEM((cells, inner), F32),
                pltpu.VMEM((2, states, CHUNKS, inner), F32),
                pltpu.VMEM((cells, inner), F32),
                pltpu.VMEM((halves, cells, LANES), F32),
                pltpu.VMEM((4 * states, cells, LANES), F32),
            ],
            compiler_params=MIDDLE,
            cost_estimate=pl.CostEstimate(
                flops=48 * 1024 * cells * inner,
                bytes_accessed=8 * cells * inner,
                transcendentals=4 * states * cells * inner,
            ),
            name="forward_scans",
        )(line, *weights)

    row_line, col_line = (exchange(embedded, "col"), exchange(turned, "row"))
    row_sums, row_starts = forward(0, row_line)
    row_sums, col_line = lax.optimization_barrier((row_sums, col_line))
    along_rows = exchange(row_sums, "col")
    col_sums, col_starts = forward(1, col_line)
    along_rows, col_sums = lax.optimization_barrier((along_rows, col_sums))
    along_cols = exchange(col_sums, "row")

    firsts = pack_sizes(inner, width, rank, states)
    gate_rows = halves * width + inner + 8
    d_rows, d_cols, d_own, gate_packed = pl.pallas_call(
        functools.partial(gate_kernel, edge=edge),
        out_shape=(
            shape_of(cells, inner),
            shape_of(cells, inner),
            shape_of(cells, width),
            shape_of(gate_rows, LANES),
        ),
        scratch_shapes=[pltpu.VMEM((halves, cells, LANES), F32)],
        compiler_params=SMALL,
        name="gate",
    )(
        embedded,
        gain,
        in_weight,
        output_gain.reshape(1, inner),
        output_weight,
        cotangent.reshape(cells, width),
        along_rows,
        along_cols,
    )

    def backward(pair, line, starts, arriving):
        return pl.pallas_call(
            functools.partial(backward_kernel, pair=pair, rank=rank, states=states),
            out_shape=(shape_of(cells, width), shape_of(firsts[5], LANES)),
            scratch_shapes=[
                pltpu.VMEM((2, cells, inner), F32),
                pltpu.VMEM((cells, inner), F32),
                pltpu.VMEM((2, states, CHUNKS, inner), F32),
                pltpu.VMEM((span + 1, states, CHUNKS, inner), F32),
                pltpu.VMEM((span, states, CHUNKS, inner), F32),
                pltpu.VMEM((cells, LANES), F32),
                pltpu.VMEM((cells, inner), F32),
                pltpu.VMEM((cells, inner), F32),
                pltpu.VMEM((states, CHUNKS, inner), F32),
                pltpu.VMEM((states, CHUNKS, inner), F32),
                pltpu.VMEM((halves, cells, LANES), F32),
                pltpu.VMEM((cells, inner), F32),
                pltpu.VMEM((4 * states, cells, LANES), F32),
                pltpu.VMEM((2 * states, cells, LANES), F32),
                pltpu.VMEM((2, cells, inner), F32),
            ],
            compiler_params=LARGE,
            cost_estimate=pl.CostEstimate(
                flops=96 * 1024 * cells * inner,
                bytes_accessed=8 * cells * inner,
                transcendentals=4 * states * cells * inner,
            ),
            name="backward_scans",
        )(line, *weights, starts, arriving)

    arriving_cols = exchange(d_cols, "row")
    arriving_rows = exchange(d_rows, "col")
    back_cols, packed_cols = backward(1, col_line, col_starts, arriving_cols)
    back_rows, packed_rows = backward(0, row_line, row_starts, arriving_rows)

    row_count, col_count = (lax.axis_size("row"), lax.axis_size("col"))
    shared = firsts[1]
    stacked_rows = gate_rows + 2 * firsts[5] - shared
    stacked_rows += -stacked_rows % (row_count * 8)
    share_rows = stacked_rows // row_count
    blocks = pl.pallas_call(
        functools.partial(pack_kernel, shared=shared),
        out_shape=shape_of(row_count, edge + share_rows, LANES),
        scratch_shapes=[pltpu.VMEM((stacked_rows, LANES), F32)],
        compiler_params=SMALL,
        name="pack",
    )(gate_packed, packed_rows, packed_cols, back_cols)
    received = lax.all_to_all(blocks, "row", 0, 0)
    partial = jnp.sum(received[:, edge:], axis=0)
    lines_back = back_rows.reshape(col_count, cells // col_count, width)
    copies = jnp.broadcast_to(partial[None], (col_count,) + partial.shape)
    crossed = lax.all_to_all(jnp.concatenate([lines_back, copies], axis=1), "col", 0, 0)
    column_sums = jnp.sum(crossed[:, across:], axis=0)
    whole = share(column_sums, "row").reshape(stacked_rows, LANES)

    feature_grad = pl.pallas_call(
        functools.partial(finish_kernel, edge=edge),
        out_shape=shape_of(cells, width, dtype=BF16),
        scratch_shapes=[pltpu.VMEM((cells, width), F32)],
        compiler_params=SMALL,
        name="finish",
    )(d_own, crossed[:, :across], received[:, :edge])
    grads = pl.pallas_call(
        functools.partial(unpack_kernel, scale=scale, rank=rank, states=states),
        out_shape=(
            shape_of(width, 2 * inner),
            shape_of(4 * group, inner),
            shape_of(4, rank, inner),
            shape_of(4, inner),
            shape_of(4, states, inner),
            shape_of(4, inner),
            shape_of(1, width),
            shape_of(1, inner),
            shape_of(inner, width),
        ),
        compiler_params=SMALL,
        name="unpack",
    )(whole)
    return (
        feature_grad.reshape(edge, across, width),
        grads[0],
        grads[1].T,
        *grads[2:6],
        grads[6].reshape(width),
        grads[7].reshape(inner),
        grads[8],
    )


def solution(mesh):
    tiled = P("row", "col", None)
    in_specs = (P("row", "col"), tiled, tiled) + (P(),) * 10
    out_specs = (tiled,) + (P(),) * 9
    return jax.shard_map(local, mesh=mesh, in_specs=in_specs, out_specs=out_specs, check_vma=False)
```
